128 devices in a mesh: ctx: 16 (over x_hi, y, core), exp: 8 (over z, x_lo).
Axes of the slice: x: 4 (x_hi: 2, x_lo: 2; x = x_hi * 2 + x_lo), y: 4, z: 4, core: 2. Of those that a mesh axis runs over, the one named last changes fastest.
Arguments:
- latent: bfloat16 [2048, 576], P('ctx'), may hold values from -8 to 8
- query: bfloat16 [2048, 12288], P('ctx', 'exp'), may hold values from -8 to 8
- w_uk: bfloat16 [64, 512, 128], P('exp'), may hold values from -0.5 to 0.5
- w_uv: bfloat16 [64, 512, 128], P('exp'), may hold values from -0.25 to 0.25
- w_o: bfloat16 [8192, 4096], P('exp'), may hold values from -0.0625 to 0.0625
- residual: bfloat16 [2048, 4096], P('ctx', 'exp'), may hold values from -16 to 16
- norm_gain: float32 [4096], P('exp'), may hold values from 0.1 to 1.9
- w_in: bfloat16 [32, 4096, 2, 2048], P('ctx', None, None, 'exp'), may hold values from -0.09375 to 0.09375
- w_out: bfloat16 [32, 2048, 4096], P('ctx', 'exp'), may hold values from -0.125 to 0.125
- routes: int32 [2048, 8], P('ctx'), may hold values from 0 to 31, all different within a row; in each aligned block of 128 rows (0 to 127, 128 to 255, ...) at most 48 rows name the same one
- gate_weights: float32 [2048, 8], P('ctx'), may hold values from 0.05 to 0.5
- doc_lengths: int32 [12], replicated, may hold values from 1 to 1152, 2048 in all
Outputs:
- mixed: bfloat16 [2048, 4096], P('ctx', 'exp')
The draws below stay inside these ranges and needn't reach their ends.
Inputs may be any that keep to these rules, and one draw needn't show every extreme that they name: `routes`: the 128 rows of one index of ctx name each expert at most 48 times in all, a bound that some block reaches.
All inputs are finite; a program needn't handle non-finite values.
Results may differ from the reference program's by a relative error of at most 0.009.
Values may be sent and summed in bfloat16 or wider, within the bound.
No kernel may reach another device: no remote copies, remote signals or barrier semaphores. Data moves between devices by JAX's collectives and lax.ppermute only.
A program may use at most 128 MiB of HBM per device.

```python
import math
import jax
import jax.numpy as jnp
import numpy as np
from jax import lax

D = 4096
HEADS = 64
NOPE = 128
ROPE = 64
LAT = 512
VDIM = 128
FF = 2048
TOP = 8
DOCS = 12
TOK = 128
SEQ = 2048
EXPERTS = 32
CAP = 48
LONGEST = 1152
N_CTX = 16
N_EXP = 8


def draw_latent(key, part):
    key = jax.random.fold_in(key, 11)
    base = jnp.clip(jax.random.normal(key, (SEQ, LAT + ROPE), jnp.float32), -8.0, 8.0)
    return base.astype(jnp.bfloat16)


def draw_query(key, part):
    key = jax.random.fold_in(key, 12)
    base = jnp.clip(jax.random.normal(key, (SEQ, HEADS, NOPE + ROPE), jnp.float32), -8.0, 8.0)
    return base.reshape(SEQ, HEADS * (NOPE + ROPE)).astype(jnp.bfloat16)


def feature_scales(key, low, ratio):
    ramp = jnp.arange(D, dtype=jnp.float32) / D
    jitter = jax.random.uniform(jax.random.fold_in(key, 5), (D,), jnp.float32, 0.7, 1.4)
    return low * jnp.power(ratio, ramp) * jitter


def draw_residual(key, part):
    key = jax.random.fold_in(key, 13)
    scales = feature_scales(key, 0.3, 10.0)
    base = jnp.clip(jax.random.normal(key, (SEQ, D), jnp.float32), -3.5, 3.5)
    return jnp.clip(base * scales[None, :], -16.0, 16.0).astype(jnp.bfloat16)


def level_of(stream_key, extent, shards, low, high):
    level, own = 1.0, jax.random.fold_in(stream_key, 6)
    for axis_at, parts in shards:
        draws = jnp.exp(jax.random.uniform(jax.random.fold_in(own, axis_at), (parts,), jnp.float32, low / len(shards), high / len(shards)))
        level = level * jnp.repeat(draws, extent[axis_at] // parts).reshape([-1 if axis == axis_at else 1 for axis in range(len(extent))])
    return level


def split_up(count, total, most, lean):
    weights = [(1 << 20) // math.isqrt(standing ** lean) + 1 for standing in range(2, count + 1)]
    rest, holding = total - most - (count - 1), [1] * (count - 1)
    while rest > 0:
        free = [i for i in range(count - 1) if holding[i] < most]
        whole, remaining = sum([weights[i] for i in free]), rest
        for i in free:
            addition = min(most - holding[i], max(1, remaining * weights[i] // whole), rest)
            holding[i] = holding[i] + addition
            rest = rest - addition
    return np.array([most] + holding)


def uneven(key, count, total, bound, skew):
    if count == 2:
        one = jax.random.randint(key, (), max(1, total - bound), min(bound, total - 1) + 1)
        return jnp.stack([one, total - one])
    sizes = jnp.asarray(split_up(count, total, bound, skew), jnp.int32)
    twos = (count - 1) // 2
    donor, receiver = sizes[1:1 + 2 * twos:2], sizes[2:2 + 2 * twos:2]
    slack = jnp.minimum(donor - 1, bound - receiver)
    shifted = jax.random.randint(jax.random.fold_in(key, 1), (twos,), 0, 1 << 20) % (slack + 1)
    sizes = sizes.at[1:1 + 2 * twos:2].set(donor - shifted).at[2:2 + 2 * twos:2].set(receiver + shifted)
    return sizes[jax.random.permutation(jax.random.fold_in(key, 2), count)]


def shared_out(stream_key, own, number, rows, number_of, top, bound, skew):
    ranking = jax.random.permutation(stream_key, number_of)
    heavy_load, ordinary = load_shares(number_of, rows * top, bound, skew, True), load_shares(number_of, rows * top, bound, skew, False)
    places = jnp.arange(number_of)

    def named(lengths, offset_by):
        used = int((lengths > 0).sum())
        fixed = max(1, used // 4)
        moved = fixed + (places - fixed + offset_by * (used - fixed)) % max(1, number_of - fixed)
        return jnp.zeros((number_of,), jnp.int32).at[ranking[jnp.where(places < fixed, places, moved)]].set(jnp.asarray(lengths, jnp.int32))

    lengths = jnp.where(number % 4 == 0, named(heavy_load, number // 4), named(ordinary, number - number // 4 - 1))
    mixed = jax.random.permutation(jax.random.fold_in(own, 3), number_of)
    donor, receiver = mixed[0:number_of // 2 * 2:2], mixed[1:number_of // 2 * 2:2]
    slack = jnp.minimum(lengths[donor] - 1, bound - lengths[receiver]) // 2
    slack = jnp.where((donor == ranking[0]) | (receiver == ranking[0]) | (lengths[receiver] == 0), 0, jnp.maximum(slack, 0))
    moved = jax.random.randint(jax.random.fold_in(own, 4), (number_of // 2,), 0, 1 << 20) % (slack + 1)
    lengths = lengths.at[donor].add(-moved).at[receiver].add(moved)
    items = jnp.searchsorted(jnp.cumsum(lengths), jnp.arange(rows * top), side="right").astype(jnp.int32)
    grid = items.reshape(top, rows).T
    grid = grid[jax.random.permutation(jax.random.fold_in(own, 1), rows)]
    offset_by = jax.random.randint(jax.random.fold_in(own, 2), (rows, 1), 0, top)
    return jnp.take_along_axis(grid, (jnp.arange(top)[None, :] + offset_by) % top, axis=1)


def load_shares(number_of, total, bound, skew, full):
    loads = [(1 << 20) // math.isqrt(grade ** skew) + 1 for grade in range(1, number_of + 1)]
    largest = bound if full else min(bound, max(-(-total // number_of), total * loads[0] // sum(loads)))
    least = 1 if total - largest >= number_of - 1 else 0
    holding, surplus = [largest] + [least] * (number_of - 1), total - largest - least * (number_of - 1)
    while surplus > 0:
        free = [i for i in range(1, number_of) if holding[i] < largest] or [i for i in range(1, number_of) if holding[i] < bound]
        whole, left = sum([loads[i] for i in free]), surplus
        for i in free:
            extra = min(bound - holding[i], max(1, left * loads[i] // whole), surplus)
            holding[i] = holding[i] + extra
            surplus = surplus - extra
    return np.array(holding)


def scatter_about(key, dims, scale, bound, split=(), held_as=jnp.bfloat16):
    values = scale * jax.random.normal(key, dims, jnp.float32)
    if split:
        values = values * level_of(key, dims, split, -0.22, 0.18)
    return jnp.clip(values, -bound, bound).astype(held_as)


def setup_inputs(seed: int = 0) -> dict:
    key_list = jax.random.split(jax.random.key(seed), 13)
    latent = draw_latent(jax.random.fold_in(key_list[12], 71), 0)
    query = draw_query(jax.random.fold_in(key_list[12], 71), 0)
    w_uk = scatter_about(key_list[2], (HEADS, LAT, NOPE), NOPE ** -0.5, 0.5, ((0, 8),))
    w_uv = scatter_about(key_list[3], (HEADS, LAT, VDIM), LAT ** -0.5, 0.25, ((0, 8),))
    w_o = scatter_about(key_list[4], (HEADS * VDIM, D), (HEADS * VDIM) ** -0.5, 0.0625, ((0, 8),))
    residual = draw_residual(jax.random.fold_in(key_list[12], 71), 0)
    norm_gain = jnp.clip(1.0 + 0.18 * jax.random.normal(key_list[6], (D,), jnp.float32), 0.1, 1.9)
    w_in = scatter_about(key_list[7], (EXPERTS, D, 2, FF), D ** -0.5, 0.09375, ((0, 16), (3, 8)))
    w_out = scatter_about(key_list[8], (EXPERTS, FF, D), FF ** -0.5, 0.125, ((0, 16), (1, 8)))
    routes_keys = jax.random.split(jax.random.fold_in(key_list[9], 1), SEQ // TOK)
    routes_turns = jax.random.permutation(jax.random.fold_in(key_list[9], 3), SEQ // TOK)
    routes = jax.vmap(lambda own, number: shared_out(jax.random.fold_in(key_list[9], 2), own, number, TOK, EXPERTS, TOP, CAP, 2))(routes_keys, routes_turns).reshape((SEQ, TOP))
    gate_weights = jnp.clip(jnp.exp(math.log(0.5) - 2.3025851 * jax.random.uniform(key_list[10], (SEQ, TOP), jnp.float32) ** level_of(key_list[10], (SEQ, TOP), ((0, 16),), -0.2, 0.2)), 0.05, 0.5)
    doc_lengths = uneven(key_list[11], DOCS, SEQ, LONGEST, 2).astype(jnp.int32)
    return dict(latent=latent, query=query, w_uk=w_uk, w_uv=w_uv, w_o=w_o, residual=residual, norm_gain=norm_gain, w_in=w_in, w_out=w_out, routes=routes, gate_weights=gate_weights, doc_lengths=doc_lengths)


def reference(latent, query, w_uk, w_uv, w_o, residual, norm_gain, w_in, w_out, routes, gate_weights, doc_lengths):
    score_scale = 1.0 / math.sqrt(NOPE + ROPE)
    positions = jnp.arange(SEQ, dtype=jnp.int32)
    doc_ends = jnp.cumsum(doc_lengths)
    doc_ids = lax.optimization_barrier(jnp.sum((positions[:, None] >= doc_ends[None, :]).astype(jnp.int32), axis=1))
    allowed = (doc_ids[:, None] == doc_ids[None, :]) & (positions[:, None] >= positions[None, :])
    q_heads = query.reshape(SEQ, HEADS, NOPE + ROPE).transpose(1, 0, 2)
    value_rows = latent[:, :LAT]

    def one_head(inputs):
        q_head, key_up, value_up = inputs
        q_lat = jnp.dot(q_head[:, :NOPE], key_up.T, preferred_element_type=jnp.float32).astype(jnp.bfloat16)
        q_full = jnp.concatenate([q_lat, q_head[:, NOPE:]], axis=1)
        scores = jnp.dot(q_full, latent.T, preferred_element_type=jnp.float32) * score_scale
        scores = jnp.where(allowed, scores, -1e+30)
        row_max = lax.optimization_barrier(jnp.max(scores, axis=1, keepdims=True))
        weights = jnp.where(allowed, jnp.exp(scores - row_max), 0.0)
        row_total = lax.optimization_barrier(jnp.sum(weights, axis=1))
        o_lat = (jnp.dot(weights.astype(jnp.bfloat16), value_rows, preferred_element_type=jnp.float32) / row_total[:, None]).astype(jnp.bfloat16)
        return jnp.dot(o_lat, value_up, preferred_element_type=jnp.float32).astype(jnp.bfloat16)
    head_stack = lax.map(one_head, (q_heads, w_uk, w_uv))
    head_out = head_stack.transpose(1, 0, 2).reshape(SEQ, HEADS * VDIM)
    hidden = residual.astype(jnp.float32) + jnp.dot(head_out, w_o, preferred_element_type=jnp.float32)
    mean_sq = lax.optimization_barrier(jnp.mean(hidden * hidden, axis=1, keepdims=True))
    normed = (hidden * lax.rsqrt(mean_sq + 1e-06) * norm_gain.astype(jnp.float32)).astype(jnp.bfloat16)
    row_limit = N_CTX * CAP

    def expert_step(moe_sum, inputs):
        expert_id, expert_in, expert_out = inputs
        hit_mask = routes == expert_id
        weight = lax.optimization_barrier(jnp.sum(jnp.where(hit_mask, gate_weights, 0.0), axis=1))
        chosen = jnp.any(hit_mask, axis=1)
        row_ids = jnp.nonzero(chosen, size=row_limit, fill_value=0)[0].astype(jnp.int32)
        live_rows = (jnp.arange(row_limit, dtype=jnp.int32) < jnp.sum(chosen.astype(jnp.int32))).astype(jnp.float32)
        picked_rows = normed[row_ids].astype(jnp.float32)
        hidden_pre = jnp.einsum('md,dgf->mgf', picked_rows, expert_in.astype(jnp.float32))
        activated = (jax.nn.silu(hidden_pre[:, 0]) * hidden_pre[:, 1]).astype(jnp.bfloat16)
        act_blocks = activated.reshape(row_limit, N_EXP, FF // N_EXP).astype(jnp.float32)
        down_blocks = expert_out.reshape(N_EXP, FF // N_EXP, D).astype(jnp.float32)
        partials = jnp.einsum('mbf,bfd->mbd', act_blocks, down_blocks).astype(jnp.bfloat16)
        block_sum = lax.optimization_barrier(jnp.sum(partials.astype(jnp.float32), axis=1))
        contrib = block_sum * (weight[row_ids] * live_rows)[:, None]
        return (moe_sum.at[row_ids].add(contrib), None)
    moe_out, _ = lax.scan(expert_step, jnp.zeros((SEQ, D), jnp.float32), (jnp.arange(EXPERTS, dtype=jnp.int32), w_in, w_out))
    return (hidden + moe_out).astype(jnp.bfloat16)
```

```python
import itertools
import math

import jax
import jax.numpy as jnp
from jax import lax
from jax.sharding import PartitionSpec as P

D = 4096
NOPE = 128
ROPE = 64
LAT = 512
VDIM = 128
TOP = 8
EXPERTS = 32
GATE_COLS = 128
BOTH = ("ctx", "exp")

epsilon = 1e-06


def table(dx=0, dy=0, dz=0, dc=0):
    def at(x, y, z, c):
        return ((x // 2 * 4 + y) * 2 + c) * 8 + z * 2 + x % 2

    return [
        (at(x, y, z, c), at((x + dx) % 4, (y + dy) % 4, (z + dz) % 4, (c + dc) % 2))
        for x, y, z, c in itertools.product(range(4), range(4), range(4), range(2))
    ]


def shift(value, axis, by):
    return lax.ppermute(value, BOTH, table(**{"d" + axis: by}))


def other_core(value):
    return shift(value, "c", 1)


def ring(block, axis):
    return [block, shift(block, axis, 1), shift(block, axis, -1), shift(block, axis, 2)]


def add_up(*blocks):
    total = blocks[0].astype(jnp.float32)
    for block in blocks[1:]:
        total = total + block.astype(jnp.float32)
    return total


def ring_sum(own, before, after, far, axis):
    return add_up(own, shift(before, axis, -1), shift(after, axis, 1), shift(far, axis, 2))


def document(positions, doc_ends):
    return jnp.sum((positions[:, None] >= doc_ends[None, :]).astype(jnp.int32), axis=1)


def attention(latent, query, w_uk, w_uv, doc_lengths):
    tokens = latent.shape[0]
    heads = w_uk.shape[0]
    qk_width = NOPE + ROPE
    score_scale = 1.0 / math.sqrt(qk_width)
    doc_ends = jnp.cumsum(doc_lengths)
    ctx = lax.axis_index("ctx")
    x_hi, y, core = ctx // 8, (ctx // 2) % 4, ctx % 2
    pair = jnp.concatenate([latent, shift(latent, "x", 2)], axis=0)
    half = jnp.concatenate(ring(pair, "y"), axis=0)
    piece = jnp.concatenate([half, other_core(half)], axis=0)
    starts = [
        (((x_hi + dx) % 2 * 4 + (y + dy) % 4) * 2 + (core + dc) % 2) * tokens
        for dc in (0, 1)
        for dy in (0, 3, 1, 2)
        for dx in (0, 1)
    ]
    steps = jnp.arange(tokens, dtype=jnp.int32)
    key_pos = (jnp.stack(starts)[:, None] + steps[None, :]).reshape(-1)
    key_doc = document(key_pos, doc_ends)
    q_pos = ctx * tokens + steps
    q_doc = document(q_pos, doc_ends)
    q_rows = query.reshape(tokens, heads, qk_width)
    q_lat = jnp.einsum(
        "thn,hln->htl", q_rows[:, :, :NOPE], w_uk, preferred_element_type=jnp.float32
    ).astype(jnp.bfloat16)
    q_full = jnp.concatenate(
        [q_lat, jnp.transpose(q_rows[:, :, NOPE:], (1, 0, 2))], axis=2
    ).reshape(heads * tokens, LAT + ROPE)
    row_pos = jnp.tile(q_pos, heads)
    row_doc = jnp.tile(q_doc, heads)
    allowed = (row_doc[:, None] == key_doc[None, :]) & (row_pos[:, None] >= key_pos[None, :])
    scores = jnp.dot(q_full, piece.T, preferred_element_type=jnp.float32) * score_scale
    scores = jnp.where(allowed, scores, -1e30)
    row_max = jnp.max(scores, axis=1)
    weights = jnp.where(allowed, jnp.exp(scores - row_max[:, None]), 0.0)
    row_total = jnp.sum(weights, axis=1)
    accumulated = jnp.dot(
        weights.astype(jnp.bfloat16), piece[:, :LAT], preferred_element_type=jnp.float32
    )
    o_lat = (accumulated / row_total[:, None]).astype(jnp.bfloat16).reshape(heads, tokens, LAT)
    return (
        jnp.einsum("htl,hlv->thv", o_lat, w_uv, preferred_element_type=jnp.float32)
        .astype(jnp.bfloat16)
        .reshape(tokens, heads * VDIM)
    )


def body(
    latent,
    query,
    w_uk,
    w_uv,
    w_o,
    residual,
    norm_gain,
    w_in,
    w_out,
    routes,
    gate_weights,
    doc_lengths,
):
    tokens = latent.shape[0]
    count_exp = lax.axis_size("exp")
    local_width = residual.shape[1]
    own = tokens // count_exp
    ctx, exp = lax.axis_index("ctx"), lax.axis_index("exp")
    local_experts = w_in.shape[0]
    units = w_in.shape[3]

    sent = jnp.concatenate(
        [
            residual.astype(jnp.float32).reshape(count_exp, own, local_width),
            jnp.broadcast_to(norm_gain[None, None, :], (count_exp, 1, local_width)),
        ],
        axis=1,
    )
    got = lax.all_to_all(sent, "exp", split_axis=0, concat_axis=0)
    wide = jnp.transpose(got, (1, 0, 2)).reshape(own + 1, D)
    residual_rows, gain = wide[:own], wide[own]

    own_routes = lax.dynamic_slice_in_dim(routes, exp * own, own, axis=0)
    own_gates = lax.dynamic_slice_in_dim(gate_weights, exp * own, own, axis=0)
    named = own_routes[:, :, None] == jnp.arange(EXPERTS, dtype=jnp.int32)[None, None, :]
    dense = jnp.sum(jnp.where(named, own_gates[:, :, None], 0.0), axis=1)
    high = dense.astype(jnp.bfloat16)
    low = (dense - high.astype(jnp.float32)).astype(jnp.bfloat16)
    gate_row = jnp.concatenate(
        [high, low, jnp.zeros((own, GATE_COLS - 2 * EXPERTS), jnp.bfloat16)], axis=1
    )
    column = jnp.arange(GATE_COLS, dtype=jnp.int32)[:, None]
    mine = ctx * local_experts + jnp.arange(local_experts, dtype=jnp.int32)[None, :]
    pick = ((column == mine) | (column == mine + EXPERTS)).astype(jnp.bfloat16)

    up = jnp.transpose(w_in, (1, 0, 2, 3)).reshape(D, local_experts * 2 * units)
    down = w_out.reshape(local_experts * units, D)

    def experts(rows):
        pre = jnp.dot(rows[:, :D], up, preferred_element_type=jnp.float32)
        gates = jnp.dot(rows[:, D:], pick, preferred_element_type=jnp.float32)
        acts = []
        for e in range(local_experts):
            gate_pre = pre[:, 2 * e * units : (2 * e + 1) * units]
            up_pre = pre[:, (2 * e + 1) * units : (2 * e + 2) * units]
            acts.append(jax.nn.silu(gate_pre) * up_pre * gates[:, e : e + 1])
        activated = jnp.concatenate(acts, axis=1).astype(jnp.bfloat16)
        return jnp.dot(activated, down, preferred_element_type=jnp.float32).astype(jnp.bfloat16)

    def both_cores(rows):
        theirs = other_core(rows)
        result = experts(jnp.concatenate([theirs, rows], axis=0))
        count = rows.shape[0]
        return add_up(result[count:], other_core(result[:count])).astype(jnp.bfloat16)

    head_out = attention(latent, query, w_uk, w_uv, doc_lengths)
    partial = jnp.dot(head_out, w_o, preferred_element_type=jnp.float32).astype(jnp.bfloat16)
    parts = lax.all_to_all(
        partial.reshape(count_exp, own, D), "exp", split_axis=0, concat_axis=0
    )
    hidden = residual_rows + jnp.sum(parts.astype(jnp.float32), axis=0)
    squares = jnp.mean(hidden * hidden, axis=1, keepdims=True)
    normed = (hidden * lax.rsqrt(squares + epsilon) * gain[None, :]).astype(jnp.bfloat16)
    rows = jnp.concatenate([normed, gate_row], axis=1)

    x_own, x_before, x_after, x_far = ring(rows, "x")
    first = jnp.concatenate(ring(jnp.concatenate([x_own, x_before], axis=0), "z"), axis=0)
    second = jnp.concatenate(ring(jnp.concatenate([x_after, x_far], axis=0), "y"), axis=0)
    count = first.shape[0]
    near = count // 2
    gathered = []
    for block, axis in ((first, "y"), (second, "z")):
        before, after = shift(block, axis, 1), shift(block, axis, -1)
        far = jnp.concatenate(
            [shift(before[:near], axis, 1), shift(after[near:], axis, -1)], axis=0
        )
        gathered.append((before, after, far))
    (y_before, y_after, y_far), (z_before, z_after, z_far) = gathered

    out_own = both_cores(jnp.concatenate([first, second], axis=0))
    out_before = both_cores(jnp.concatenate([y_before, z_before], axis=0))
    out_after = both_cores(jnp.concatenate([y_after, z_after], axis=0))
    out_far = both_cores(jnp.concatenate([y_far, z_far], axis=0))

    first = ring_sum(*[o[:count] for o in (out_own, out_before, out_after, out_far)], "y")
    second = ring_sum(*[o[count:] for o in (out_own, out_before, out_after, out_far)], "z")
    first, second = first.astype(jnp.bfloat16), second.astype(jnp.bfloat16)
    pair = 2 * own
    first = ring_sum(*[first[i * pair : (i + 1) * pair] for i in range(4)], "z")
    second = ring_sum(*[second[i * pair : (i + 1) * pair] for i in range(4)], "y")
    first, second = first.astype(jnp.bfloat16), second.astype(jnp.bfloat16)
    moe_out = ring_sum(first[:own], first[own:], second[:own], second[own:], "x")
    mixed = (hidden + moe_out).astype(jnp.bfloat16)
    return lax.all_to_all(mixed, "exp", split_axis=1, concat_axis=0, tiled=True)


def solution(mesh):
    placed = (
        P("ctx", None),
        P("ctx", "exp"),
        P("exp", None, None),
        P("exp", None, None),
        P("exp", None),
        P("ctx", "exp"),
        P("exp"),
        P("ctx", None, None, "exp"),
        P("ctx", "exp", None),
        P("ctx", None),
        P("ctx", None),
        P(),
    )
    return jax.shard_map(
        body, mesh=mesh, in_specs=placed, out_specs=P("ctx", "exp"), check_vma=False
    )
```

```python
import functools
import itertools
import math

import jax
import jax.numpy as jnp
from jax import lax
from jax.experimental import pallas as pl
from jax.experimental.pallas import tpu as pltpu
from jax.sharding import PartitionSpec as P

D = 4096
NOPE = 128
ROPE = 64
LAT = 512
VDIM = 128
TOP = 8
EXPERTS = 32
GATE_COLS = 128
BOTH = ("ctx", "exp")

epsilon = 1e-06


def table(dx=0, dy=0, dz=0, dc=0):
    def at(x, y, z, c):
        return ((x // 2 * 4 + y) * 2 + c) * 8 + z * 2 + x % 2

    return [
        (at(x, y, z, c), at((x + dx) % 4, (y + dy) % 4, (z + dz) % 4, (c + dc) % 2))
        for x, y, z, c in itertools.product(range(4), range(4), range(4), range(2))
    ]


def shift(value, axis, by):
    return lax.ppermute(value, BOTH, table(**{"d" + axis: by}))


def other_core(value):
    return shift(value, "c", 1)


def ring(block, axis):
    return [block, shift(block, axis, 1), shift(block, axis, -1), shift(block, axis, 2)]


def add_up(*blocks):
    total = blocks[0].astype(jnp.float32)
    for block in blocks[1:]:
        total = total + block.astype(jnp.float32)
    return total


def ring_sum(own, before, after, far, axis):
    return add_up(own, shift(before, axis, -1), shift(after, axis, 1), shift(far, axis, 2))


VMEM_LIMIT = 56 * 1024 * 1024


def grouped(refs, sizes):
    found, at = [], 0
    for size in sizes:
        found.append(refs[at : at + size])
        at += size
    return found


def stack_kernel(sizes, *refs):
    count = sum(sizes)
    for group, out in zip(grouped(refs[:count], sizes), refs[count:]):
        at = 0
        for ref in group:
            out[at : at + ref.shape[0], :] = ref[...]
            at += ref.shape[0]


def stack(*groups):
    sizes = tuple(len(group) for group in groups)
    blocks = [block for group in groups for block in group]
    width = blocks[0].shape[1]
    heights = [sum(block.shape[0] for block in group) for group in groups]
    tile = width // 3
    return pl.pallas_call(
        functools.partial(stack_kernel, sizes),
        grid=(3,),
        in_specs=[pl.BlockSpec((block.shape[0], tile), lambda i: (0, i)) for block in blocks],
        out_specs=[pl.BlockSpec((height, tile), lambda i: (0, i)) for height in heights],
        out_shape=[jax.ShapeDtypeStruct((height, width), jnp.bfloat16) for height in heights],
        compiler_params=pltpu.CompilerParams(vmem_limit_bytes=VMEM_LIMIT),
        cost_estimate=pl.CostEstimate(
            flops=0, bytes_accessed=4 * sum(heights) * width, transcendentals=0
        ),
    )(*blocks)


def sums_kernel(sizes, *refs):
    count = sum(sizes)
    outs = refs[count:]
    parts = len(outs) // len(sizes)
    for at, group in enumerate(grouped(refs[:count], sizes)):
        total = group[0][...].astype(jnp.float32)
        for ref in group[1:]:
            total = total + ref[...].astype(jnp.float32)
        total = total.astype(jnp.bfloat16)
        rows = total.shape[0] // parts
        for part in range(parts):
            outs[at * parts + part][...] = total[part * rows : (part + 1) * rows]


def sums(parts, *groups):
    sizes = tuple(len(group) for group in groups)
    blocks = [block for group in groups for block in group]
    width = blocks[0].shape[1]
    heights = [group[0].shape[0] // parts for group in groups for _ in range(parts)]
    tile = width // 4
    outs = pl.pallas_call(
        functools.partial(sums_kernel, sizes),
        grid=(4,),
        in_specs=[pl.BlockSpec((block.shape[0], tile), lambda i: (0, i)) for block in blocks],
        out_specs=[pl.BlockSpec((height, tile), lambda i: (0, i)) for height in heights],
        out_shape=[jax.ShapeDtypeStruct((height, width), jnp.bfloat16) for height in heights],
        compiler_params=pltpu.CompilerParams(vmem_limit_bytes=VMEM_LIMIT),
        cost_estimate=pl.CostEstimate(
            flops=0,
            bytes_accessed=2 * width * (sum(heights) + sum(b.shape[0] for b in blocks)),
            transcendentals=0,
        ),
    )(*blocks)
    return grouped(outs, [parts] * len(groups))


STEPS = 4


def experts_kernel(sizes, *refs):
    count = sum(sizes)
    blocks, gate_refs = refs[:count], refs[count : 2 * count]
    up, down, pick = refs[2 * count : 2 * count + 3]
    outs = refs[2 * count + 3 : 2 * count + 3 + len(sizes)]
    pre, act = refs[2 * count + 3 + len(sizes) :]
    step = pl.program_id(0)
    units = up.shape[3]

    @pl.when(step < STEPS)
    def _():
        rows = jnp.concatenate([block[...] for block in blocks], axis=0)
        for e in range(up.shape[0]):
            for g in range(2):
                columns = slice((2 * e + g) * units, (2 * e + g + 1) * units)
                product = jnp.dot(rows, up[e, g], preferred_element_type=jnp.float32)

                @pl.when(step == 0)
                def _():
                    pre[:, columns] = product

                @pl.when(step > 0)
                def _():
                    pre[:, columns] += product

    @pl.when(step == STEPS - 1)
    def _():
        gate_rows = jnp.concatenate([ref[...] for ref in gate_refs], axis=0)
        gates = jnp.dot(gate_rows, pick[...], preferred_element_type=jnp.float32)
        for e in range(up.shape[0]):
            gate_pre = pre[:, 2 * e * units : (2 * e + 1) * units]
            up_pre = pre[:, (2 * e + 1) * units : (2 * e + 2) * units]
            value = gate_pre / (1.0 + jnp.exp(-gate_pre)) * up_pre * gates[:, e : e + 1]
            act[:, e * units : (e + 1) * units] = value.astype(jnp.bfloat16)

    @pl.when(step >= STEPS)
    def _():
        result = jnp.dot(act[...], down[...], preferred_element_type=jnp.float32).astype(
            jnp.bfloat16
        )
        at = 0
        for out in outs:
            out[...] = result[at : at + out.shape[0]]
            at += out.shape[0]


def run_experts(groups, up, down, pick):
    sizes = tuple(len(group) for group in groups)
    blocks = [block for group in groups for block in group]
    heights = [sum(block.shape[0] for block in group) for group in groups]
    height = sum(heights)
    experts, _, _, units = up.shape
    tile = D // STEPS
    early = lambda i: jnp.minimum(i, STEPS - 1)
    late = lambda i: jnp.maximum(i - STEPS, 0)
    return pl.pallas_call(
        functools.partial(experts_kernel, sizes),
        grid=(2 * STEPS,),
        in_specs=[pl.BlockSpec((b.shape[0], tile), lambda i: (0, early(i))) for b in blocks]
        + [pl.BlockSpec((b.shape[0], GATE_COLS), lambda i: (0, D // GATE_COLS)) for b in blocks]
        + [
            pl.BlockSpec((experts, 2, tile, units), lambda i: (0, 0, early(i), 0)),
            pl.BlockSpec((experts * units, tile), lambda i: (0, late(i))),
            pl.BlockSpec(pick.shape, lambda i: (0, 0)),
        ],
        out_specs=[pl.BlockSpec((h, tile), lambda i: (0, late(i))) for h in heights],
        out_shape=[jax.ShapeDtypeStruct((h, D), jnp.bfloat16) for h in heights],
        scratch_shapes=[
            pltpu.VMEM((height, experts * 2 * units), jnp.float32),
            pltpu.VMEM((height, experts * units), jnp.bfloat16),
        ],
        compiler_params=pltpu.CompilerParams(vmem_limit_bytes=VMEM_LIMIT),
        cost_estimate=pl.CostEstimate(
            flops=6 * height * D * experts * units,
            bytes_accessed=6 * experts * units * D + 4 * height * D,
            transcendentals=height * experts * units,
        ),
    )(*blocks, *blocks, up, down, pick)


def document(positions, doc_ends):
    return jnp.sum((positions[:, None] >= doc_ends[None, :]).astype(jnp.int32), axis=1)


def attention(latent, query, w_uk, w_uv, doc_lengths, up):
    tokens = latent.shape[0]
    heads = w_uk.shape[0]
    qk_width = NOPE + ROPE
    score_scale = 1.0 / math.sqrt(qk_width)
    doc_ends = jnp.cumsum(doc_lengths)
    ctx = lax.axis_index("ctx")
    x_hi, y, core = ctx // 8, (ctx // 2) % 4, ctx % 2
    pair = jnp.concatenate([latent, shift(latent, "x", 2)], axis=0)
    half = jnp.concatenate(ring(pair, "y"), axis=0)
    piece = jnp.concatenate([half, other_core(half)], axis=0)
    piece, up = lax.optimization_barrier((piece, up))
    starts = [
        (((x_hi + dx) % 2 * 4 + (y + dy) % 4) * 2 + (core + dc) % 2) * tokens
        for dc in (0, 1)
        for dy in (0, 3, 1, 2)
        for dx in (0, 1)
    ]
    steps = jnp.arange(tokens, dtype=jnp.int32)
    key_pos = (jnp.stack(starts)[:, None] + steps[None, :]).reshape(-1)
    key_doc = document(key_pos, doc_ends)
    q_pos = ctx * tokens + steps
    q_doc = document(q_pos, doc_ends)
    q_rows = query.reshape(tokens, heads, qk_width)
    q_lat = jnp.einsum(
        "thn,hln->htl", q_rows[:, :, :NOPE], w_uk, preferred_element_type=jnp.float32
    ).astype(jnp.bfloat16)
    q_full = jnp.concatenate(
        [q_lat, jnp.transpose(q_rows[:, :, NOPE:], (1, 0, 2))], axis=2
    ).reshape(heads * tokens, LAT + ROPE)
    row_pos = jnp.tile(q_pos, heads)
    row_doc = jnp.tile(q_doc, heads)
    allowed = (row_doc[:, None] == key_doc[None, :]) & (row_pos[:, None] >= key_pos[None, :])
    scores = jnp.dot(q_full, piece.T, preferred_element_type=jnp.float32) * score_scale
    scores = jnp.where(allowed, scores, -1e30)
    row_max = jnp.max(scores, axis=1)
    weights = jnp.where(allowed, jnp.exp(scores - row_max[:, None]), 0.0)
    row_total = jnp.sum(weights, axis=1)
    accumulated = jnp.dot(
        weights.astype(jnp.bfloat16), piece[:, :LAT], preferred_element_type=jnp.float32
    )
    o_lat = (accumulated / row_total[:, None]).astype(jnp.bfloat16).reshape(heads, tokens, LAT)
    head_out = (
        jnp.einsum("htl,hlv->thv", o_lat, w_uv, preferred_element_type=jnp.float32)
        .astype(jnp.bfloat16)
        .reshape(tokens, heads * VDIM)
    )
    return head_out, up


def body(
    latent,
    query,
    w_uk,
    w_uv,
    w_o,
    residual,
    norm_gain,
    w_in,
    w_out,
    routes,
    gate_weights,
    doc_lengths,
):
    tokens = latent.shape[0]
    count_exp = lax.axis_size("exp")
    local_width = residual.shape[1]
    own = tokens // count_exp
    ctx, exp = lax.axis_index("ctx"), lax.axis_index("exp")
    local_experts = w_in.shape[0]
    units = w_in.shape[3]

    sent = jnp.concatenate(
        [
            residual.astype(jnp.float32).reshape(count_exp, own, local_width),
            jnp.broadcast_to(norm_gain[None, None, :], (count_exp, 1, local_width)),
        ],
        axis=1,
    )
    got = lax.all_to_all(sent, "exp", split_axis=0, concat_axis=0)
    wide = jnp.transpose(got, (1, 0, 2)).reshape(own + 1, D)
    residual_rows, gain = wide[:own], wide[own]

    own_routes = lax.dynamic_slice_in_dim(routes, exp * own, own, axis=0)
    own_gates = lax.dynamic_slice_in_dim(gate_weights, exp * own, own, axis=0)
    named = own_routes[:, :, None] == jnp.arange(EXPERTS, dtype=jnp.int32)[None, None, :]
    dense = jnp.sum(jnp.where(named, own_gates[:, :, None], 0.0), axis=1)
    high = dense.astype(jnp.bfloat16)
    low = (dense - high.astype(jnp.float32)).astype(jnp.bfloat16)
    gate_row = jnp.concatenate(
        [high, low, jnp.zeros((own, GATE_COLS - 2 * EXPERTS), jnp.bfloat16)], axis=1
    )
    column = jnp.arange(GATE_COLS, dtype=jnp.int32)[:, None]
    mine = ctx * local_experts + jnp.arange(local_experts, dtype=jnp.int32)[None, :]
    pick = ((column == mine) | (column == mine + EXPERTS)).astype(jnp.bfloat16)

    up = jnp.transpose(w_in, (0, 2, 1, 3))
    down = w_out.reshape(local_experts * units, D)

    def both_cores(groups):
        theirs = [[other_core(block) for block in group] for group in groups]
        result = run_experts(theirs + groups, up, down, pick)
        back = [other_core(block) for block in result[: len(groups)]]
        return [total for (total,) in sums(1, *zip(result[len(groups) :], back))]

    head_out, up = attention(latent, query, w_uk, w_uv, doc_lengths, up)
    partial = jnp.dot(head_out, w_o, preferred_element_type=jnp.float32).astype(jnp.bfloat16)
    parts = lax.all_to_all(
        partial.reshape(count_exp, own, D), "exp", split_axis=0, concat_axis=0
    )
    hidden = residual_rows + jnp.sum(parts.astype(jnp.float32), axis=0)
    squares = jnp.mean(hidden * hidden, axis=1, keepdims=True)
    normed = (hidden * lax.rsqrt(squares + epsilon) * gain[None, :]).astype(jnp.bfloat16)
    rows = jnp.concatenate([normed, gate_row], axis=1)

    x_own, x_before, x_after, x_far = ring(rows, "x")
    first, second = stack([x_own, x_before], [x_after, x_far])
    first, second = stack(ring(first, "z"), ring(second, "y"))
    near = first.shape[0] // 2
    before, after, far = [], [], []
    for block, axis in ((first, "y"), (second, "z")):
        before.append([shift(block, axis, 1)])
        after.append([shift(block, axis, -1)])
    for i, axis in enumerate("yz"):
        far.append(
            [shift(before[i][0][:near], axis, 1), shift(after[i][0][near:], axis, -1)]
        )

    first_own, second_own = both_cores([[first], [second]])
    first_before, second_before = both_cores(before)
    first_after, second_after = both_cores(after)
    first_far, second_far = both_cores(far)

    def spread(own, before, after, far, axis):
        return [own, shift(before, axis, -1), shift(after, axis, 1), shift(far, axis, 2)]

    first, second = sums(
        4,
        spread(first_own, first_before, first_after, first_far, "y"),
        spread(second_own, second_before, second_after, second_far, "z"),
    )
    first, second = sums(2, spread(*first, "z"), spread(*second, "y"))
    moe_out = ring_sum(*first, *second, "x")
    mixed = (hidden + moe_out).astype(jnp.bfloat16)
    return lax.all_to_all(mixed, "exp", split_axis=1, concat_axis=0, tiled=True)


def solution(mesh):
    placed = (
        P("ctx", None),
        P("ctx", "exp"),
        P("exp", None, None),
        P("exp", None, None),
        P("exp", None),
        P("ctx", "exp"),
        P("exp"),
        P("ctx", None, None, "exp"),
        P("ctx", "exp", None),
        P("ctx", None),
        P("ctx", None),
        P(),
    )
    return jax.shard_map(
        body, mesh=mesh, in_specs=placed, out_specs=P("ctx", "exp"), check_vma=False
    )
```

```python
import functools
import itertools
import math

import jax
import jax.numpy as jnp
from jax import lax
from jax.experimental import pallas as pl
from jax.experimental.pallas import tpu as pltpu
from jax.sharding import PartitionSpec as P

D = 4096
NOPE = 128
ROPE = 64
LAT = 512
VDIM = 128
TOP = 8
EXPERTS = 32
GATE_COLS = 128
BOTH = ("ctx", "exp")

epsilon = 1e-06


def table(dx=0, dy=0, dz=0, dc=0):
    def at(x, y, z, c):
        return ((x // 2 * 4 + y) * 2 + c) * 8 + z * 2 + x % 2

    return [
        (at(x, y, z, c), at((x + dx) % 4, (y + dy) % 4, (z + dz) % 4, (c + dc) % 2))
        for x, y, z, c in itertools.product(range(4), range(4), range(4), range(2))
    ]


def shift(value, axis, by):
    return lax.ppermute(value, BOTH, table(**{"d" + axis: by}))


def other_core(value):
    return shift(value, "c", 1)


def ring(block, axis):
    return [block, shift(block, axis, 1), shift(block, axis, -1), shift(block, axis, 2)]


def add_up(*blocks):
    total = blocks[0].astype(jnp.float32)
    for block in blocks[1:]:
        total = total + block.astype(jnp.float32)
    return total


def ring_sum(own, before, after, far, axis):
    return add_up(own, shift(before, axis, -1), shift(after, axis, 1), shift(far, axis, 2))


MIB = 1024 * 1024


def grouped(refs, sizes):
    found, at = [], 0
    for size in sizes:
        found.append(refs[at : at + size])
        at += size
    return found


def stack_kernel(sizes, *refs):
    count = sum(sizes)
    for group, out in zip(grouped(refs[:count], sizes), refs[count:]):
        at = 0
        for ref in group:
            out[at : at + ref.shape[0], :] = ref[...]
            at += ref.shape[0]


def stack(*groups):
    sizes = tuple(len(group) for group in groups)
    blocks = [block for group in groups for block in group]
    width = blocks[0].shape[1]
    heights = [sum(block.shape[0] for block in group) for group in groups]
    tile = width // 3
    return pl.pallas_call(
        functools.partial(stack_kernel, sizes),
        grid=(3,),
        in_specs=[pl.BlockSpec((block.shape[0], tile), lambda i: (0, i)) for block in blocks],
        out_specs=[pl.BlockSpec((height, tile), lambda i: (0, i)) for height in heights],
        out_shape=[jax.ShapeDtypeStruct((height, width), jnp.bfloat16) for height in heights],
        compiler_params=pltpu.CompilerParams(vmem_limit_bytes=16 * MIB),
        cost_estimate=pl.CostEstimate(
            flops=0, bytes_accessed=4 * sum(heights) * width, transcendentals=0
        ),
    )(*blocks)


STEPS = 2


def experts_kernel(sizes, *refs):
    count = sum(sizes)
    blocks, gate_refs = refs[:count], refs[count : 2 * count]
    up, down, pick = refs[2 * count : 2 * count + 3]
    outs = refs[2 * count + 3 : 2 * count + 3 + len(sizes)]
    pre, act = refs[2 * count + 3 + len(sizes) :]
    step = pl.program_id(0)
    units = up.shape[3]

    @pl.when(step == 0)
    def _():
        pre[...] = jnp.zeros_like(pre)

    @pl.when(step < STEPS)
    def _():
        rows = jnp.concatenate([block[...] for block in blocks], axis=0)
        weights = jnp.concatenate(
            [up[e, g] for e in range(up.shape[0]) for g in range(2)], axis=1
        )
        pre[...] += jnp.dot(rows, weights, preferred_element_type=jnp.float32)

    @pl.when(step == STEPS - 1)
    def _():
        gate_rows = jnp.concatenate([ref[...] for ref in gate_refs], axis=0)
        gates = jnp.dot(gate_rows, pick[...], preferred_element_type=jnp.float32)
        for e in range(up.shape[0]):
            gate_pre = pre[:, 2 * e * units : (2 * e + 1) * units]
            up_pre = pre[:, (2 * e + 1) * units : (2 * e + 2) * units]
            value = gate_pre / (1.0 + jnp.exp(-gate_pre)) * up_pre * gates[:, e : e + 1]
            act[:, e * units : (e + 1) * units] = value.astype(jnp.bfloat16)

    @pl.when(step >= STEPS)
    def _():
        result = jnp.dot(act[...], down[...], preferred_element_type=jnp.float32).astype(
            jnp.bfloat16
        )
        at = 0
        for out in outs:
            out[...] = result[at : at + out.shape[0]]
            at += out.shape[0]


def run_experts(groups, up, down, pick):
    sizes = tuple(len(group) for group in groups)
    blocks = [block for group in groups for block in group]
    heights = [sum(block.shape[0] for block in group) for group in groups]
    height = sum(heights)
    experts, _, _, units = up.shape
    tile = D // STEPS
    early = lambda i: jnp.minimum(i, STEPS - 1)
    late = lambda i: jnp.maximum(i - STEPS, 0)
    return pl.pallas_call(
        functools.partial(experts_kernel, sizes),
        grid=(2 * STEPS,),
        in_specs=[pl.BlockSpec((b.shape[0], tile), lambda i: (0, early(i))) for b in blocks]
        + [pl.BlockSpec((b.shape[0], GATE_COLS), lambda i: (0, D // GATE_COLS)) for b in blocks]
        + [
            pl.BlockSpec((experts, 2, tile, units), lambda i: (0, 0, early(i), 0)),
            pl.BlockSpec((experts * units, tile), lambda i: (0, late(i))),
            pl.BlockSpec(pick.shape, lambda i: (0, 0)),
        ],
        out_specs=[pl.BlockSpec((h, tile), lambda i: (0, late(i))) for h in heights],
        out_shape=[jax.ShapeDtypeStruct((h, D), jnp.bfloat16) for h in heights],
        scratch_shapes=[
            pltpu.VMEM((height, experts * 2 * units), jnp.float32),
            pltpu.VMEM((height, experts * units), jnp.bfloat16),
        ],
        compiler_params=pltpu.CompilerParams(vmem_limit_bytes=40 * MIB),
        cost_estimate=pl.CostEstimate(
            flops=0, bytes_accessed=4096, transcendentals=0
        ),
    )(*blocks, *blocks, up, down, pick)


def document(positions, doc_ends):
    return jnp.sum((positions[:, None] >= doc_ends[None, :]).astype(jnp.int32), axis=1)


def attention(latent, query, w_uk, w_uv, doc_lengths):
    tokens = latent.shape[0]
    heads = w_uk.shape[0]
    qk_width = NOPE + ROPE
    score_scale = 1.0 / math.sqrt(qk_width)
    doc_ends = jnp.cumsum(doc_lengths)
    ctx = lax.axis_index("ctx")
    x_hi, y, core = ctx // 8, (ctx // 2) % 4, ctx % 2
    pair = jnp.concatenate([latent, shift(latent, "x", 2)], axis=0)
    half = jnp.concatenate(ring(pair, "y"), axis=0)
    piece = jnp.concatenate([half, other_core(half)], axis=0)
    starts = [
        (((x_hi + dx) % 2 * 4 + (y + dy) % 4) * 2 + (core + dc) % 2) * tokens
        for dc in (0, 1)
        for dy in (0, 3, 1, 2)
        for dx in (0, 1)
    ]
    steps = jnp.arange(tokens, dtype=jnp.int32)
    key_pos = (jnp.stack(starts)[:, None] + steps[None, :]).reshape(-1)
    key_doc = document(key_pos, doc_ends)
    q_pos = ctx * tokens + steps
    q_doc = document(q_pos, doc_ends)
    q_rows = query.reshape(tokens, heads, qk_width)
    q_lat = jnp.einsum(
        "thn,hln->htl", q_rows[:, :, :NOPE], w_uk, preferred_element_type=jnp.float32
    ).astype(jnp.bfloat16)
    q_full = jnp.concatenate(
        [q_lat, jnp.transpose(q_rows[:, :, NOPE:], (1, 0, 2))], axis=2
    ).reshape(heads * tokens, LAT + ROPE)
    row_pos = jnp.tile(q_pos, heads)
    row_doc = jnp.tile(q_doc, heads)
    allowed = (row_doc[:, None] == key_doc[None, :]) & (row_pos[:, None] >= key_pos[None, :])
    scores = jnp.dot(q_full, piece.T, preferred_element_type=jnp.float32) * score_scale
    scores = jnp.where(allowed, scores, -1e30)
    row_max = jnp.max(scores, axis=1)
    weights = jnp.where(allowed, jnp.exp(scores - row_max[:, None]), 0.0)
    row_total = jnp.sum(weights, axis=1)
    accumulated = jnp.dot(
        weights.astype(jnp.bfloat16), piece[:, :LAT], preferred_element_type=jnp.float32
    )
    o_lat = (accumulated / row_total[:, None]).astype(jnp.bfloat16).reshape(heads, tokens, LAT)
    head_out = (
        jnp.einsum("htl,hlv->thv", o_lat, w_uv, preferred_element_type=jnp.float32)
        .astype(jnp.bfloat16)
        .reshape(tokens, heads * VDIM)
    )
    return head_out


def body(
    latent,
    query,
    w_uk,
    w_uv,
    w_o,
    residual,
    norm_gain,
    w_in,
    w_out,
    routes,
    gate_weights,
    doc_lengths,
):
    tokens = latent.shape[0]
    count_exp = lax.axis_size("exp")
    local_width = residual.shape[1]
    own = tokens // count_exp
    ctx, exp = lax.axis_index("ctx"), lax.axis_index("exp")
    local_experts = w_in.shape[0]
    units = w_in.shape[3]

    sent = jnp.concatenate(
        [
            residual.astype(jnp.float32).reshape(count_exp, own, local_width),
            jnp.broadcast_to(norm_gain[None, None, :], (count_exp, 1, local_width)),
        ],
        axis=1,
    )
    got = lax.all_to_all(sent, "exp", split_axis=0, concat_axis=0)
    wide = jnp.transpose(got, (1, 0, 2)).reshape(own + 1, D)
    residual_rows, gain = wide[:own], wide[own]

    own_routes = lax.dynamic_slice_in_dim(routes, exp * own, own, axis=0)
    own_gates = lax.dynamic_slice_in_dim(gate_weights, exp * own, own, axis=0)
    named = own_routes[:, :, None] == jnp.arange(EXPERTS, dtype=jnp.int32)[None, None, :]
    dense = jnp.sum(jnp.where(named, own_gates[:, :, None], 0.0), axis=1)
    high = dense.astype(jnp.bfloat16)
    low = (dense - high.astype(jnp.float32)).astype(jnp.bfloat16)
    gate_row = jnp.concatenate(
        [high, low, jnp.zeros((own, GATE_COLS - 2 * EXPERTS), jnp.bfloat16)], axis=1
    )
    column = jnp.arange(GATE_COLS, dtype=jnp.int32)[:, None]
    mine = ctx * local_experts + jnp.arange(local_experts, dtype=jnp.int32)[None, :]
    pick = ((column == mine) | (column == mine + EXPERTS)).astype(jnp.bfloat16)

    up = jnp.transpose(w_in, (0, 2, 1, 3))
    down = w_out.reshape(local_experts * units, D)

    def own_and_theirs(groups):
        theirs = [[other_core(block) for block in group] for group in groups]
        return run_experts(theirs + groups, up, down, pick)

    def both_cores(result):
        half = len(result) // 2
        return [
            add_up(here, other_core(there)).astype(jnp.bfloat16)
            for there, here in zip(result[:half], result[half:])
        ]

    head_out = attention(latent, query, w_uk, w_uv, doc_lengths)
    partial = jnp.dot(head_out, w_o, preferred_element_type=jnp.float32).astype(jnp.bfloat16)
    parts = lax.all_to_all(
        partial.reshape(count_exp, own, D), "exp", split_axis=0, concat_axis=0
    )
    parts, up = lax.optimization_barrier((parts, up))
    hidden = residual_rows + jnp.sum(parts.astype(jnp.float32), axis=0)
    squares = jnp.mean(hidden * hidden, axis=1, keepdims=True)
    normed = (hidden * lax.rsqrt(squares + epsilon) * gain[None, :]).astype(jnp.bfloat16)
    rows = jnp.concatenate([normed, gate_row], axis=1)

    x_own, x_before, x_after, x_far = ring(rows, "x")
    first, second = stack([x_own, x_before], [x_after, x_far])
    first, second = stack(ring(first, "z"), ring(second, "y"))
    near = first.shape[0] // 2
    before, after = [], []
    for block, axis in ((first, "y"), (second, "z")):
        before.append([shift(block, axis, 1)])
        after.append([shift(block, axis, -1)])
    at_own = own_and_theirs([[first], [second]])
    before, after, at_own = lax.optimization_barrier((before, after, at_own))
    far = [
        [shift(before[i][0][:near], axis, 1), shift(after[i][0][near:], axis, -1)]
        for i, axis in enumerate("yz")
    ]
    at_before = own_and_theirs(before)
    at_after = own_and_theirs(after)
    far, at_before, at_after = lax.optimization_barrier((far, at_before, at_after))
    sum_own = both_cores(at_own)
    sum_before = both_cores(at_before)
    sum_after = both_cores(at_after)
    sent = [
        (shift(sum_before[i], axis, -1), shift(sum_after[i], axis, 1))
        for i, axis in enumerate("yz")
    ]
    sent, at_far = lax.optimization_barrier((sent, own_and_theirs(far)))
    sum_far = both_cores(at_far)
    first, second = [
        add_up(sum_own[i], *sent[i], shift(sum_far[i], axis, 2)).astype(jnp.bfloat16)
        for i, axis in enumerate("yz")
    ]
    pair = 2 * own
    first = ring_sum(*[first[i * pair : (i + 1) * pair] for i in range(4)], "z")
    second = ring_sum(*[second[i * pair : (i + 1) * pair] for i in range(4)], "y")
    first, second = first.astype(jnp.bfloat16), second.astype(jnp.bfloat16)
    moe_out = ring_sum(first[:own], first[own:], second[:own], second[own:], "x")
    mixed = (hidden + moe_out).astype(jnp.bfloat16)
    return lax.all_to_all(mixed, "exp", split_axis=1, concat_axis=0, tiled=True)


def solution(mesh):
    placed = (
        P("ctx", None),
        P("ctx", "exp"),
        P("exp", None, None),
        P("exp", None, None),
        P("exp", None),
        P("ctx", "exp"),
        P("exp"),
        P("ctx", None, None, "exp"),
        P("ctx", "exp", None),
        P("ctx", None),
        P("ctx", None),
        P(),
    )
    return jax.shard_map(
        body, mesh=mesh, in_specs=placed, out_specs=P("ctx", "exp"), check_vma=False
    )
```

```python
import functools
import itertools
import math

import jax
import jax.numpy as jnp
from jax import lax
from jax.experimental import pallas as pl
from jax.experimental.pallas import tpu as pltpu
from jax.sharding import PartitionSpec as P

D = 4096
NOPE = 128
ROPE = 64
LAT = 512
VDIM = 128
TOP = 8
EXPERTS = 32
GATE_COLS = 128
BOTH = ("ctx", "exp")
NOWHERE = 64

epsilon = 1e-06


def table(dx=0, dy=0, dz=0, dc=0):
    def at(x, y, z, c):
        return ((x // 2 * 4 + y) * 2 + c) * 8 + z * 2 + x % 2

    return [
        (at(x, y, z, c), at((x + dx) % 4, (y + dy) % 4, (z + dz) % 4, (c + dc) % 2))
        for x, y, z, c in itertools.product(range(4), range(4), range(4), range(2))
    ]


def shift(value, axis, by):
    return lax.ppermute(value, BOTH, table(**{"d" + axis: by}))


def other_core(value):
    return shift(value, "c", 1)


def ring(block, axis):
    return [block, shift(block, axis, 1), shift(block, axis, -1), shift(block, axis, 2)]


def add_up(*blocks):
    total = blocks[0].astype(jnp.float32)
    for block in blocks[1:]:
        total = total + block.astype(jnp.float32)
    return total


def ring_sum(own, before, after, far, axis):
    return add_up(own, shift(before, axis, -1), shift(after, axis, 1), shift(far, axis, 2))


MIB = 1024 * 1024


def grouped(refs, sizes):
    found, at = [], 0
    for size in sizes:
        found.append(refs[at : at + size])
        at += size
    return found


def stack_kernel(sizes, *refs):
    count = sum(sizes)
    for group, out in zip(grouped(refs[:count], sizes), refs[count:]):
        at = 0
        for ref in group:
            out[at : at + ref.shape[0], :] = ref[...]
            at += ref.shape[0]


def stack(*groups):
    sizes = tuple(len(group) for group in groups)
    blocks = [block for group in groups for block in group]
    width = blocks[0].shape[1]
    heights = [sum(block.shape[0] for block in group) for group in groups]
    cuts = 3 if width % 384 == 0 else 1
    tile = width // cuts
    return pl.pallas_call(
        functools.partial(stack_kernel, sizes),
        grid=(cuts,),
        in_specs=[pl.BlockSpec((block.shape[0], tile), lambda i: (0, i)) for block in blocks],
        out_specs=[pl.BlockSpec((height, tile), lambda i: (0, i)) for height in heights],
        out_shape=[jax.ShapeDtypeStruct((height, width), jnp.bfloat16) for height in heights],
        compiler_params=pltpu.CompilerParams(vmem_limit_bytes=16 * MIB),
        cost_estimate=pl.CostEstimate(
            flops=0, bytes_accessed=4 * sum(heights) * width, transcendentals=0
        ),
    )(*blocks)


STEPS = 2


def experts_kernel(sizes, *refs):
    count = sum(sizes)
    blocks, gate_refs = refs[:count], refs[count : 2 * count]
    up, down, pick = refs[2 * count : 2 * count + 3]
    outs = refs[2 * count + 3 : 2 * count + 3 + len(sizes)]
    pre, act = refs[2 * count + 3 + len(sizes) :]
    step = pl.program_id(0)
    units = up.shape[3]

    @pl.when(step == 0)
    def _():
        pre[...] = jnp.zeros_like(pre)

    @pl.when(step < STEPS)
    def _():
        rows = jnp.concatenate([block[...] for block in blocks], axis=0)
        weights = jnp.concatenate(
            [up[e, g] for e in range(up.shape[0]) for g in range(2)], axis=1
        )
        pre[...] += jnp.dot(rows, weights, preferred_element_type=jnp.float32)

    @pl.when(step == STEPS - 1)
    def _():
        gate_rows = jnp.concatenate([ref[...] for ref in gate_refs], axis=0)
        gates = jnp.dot(gate_rows, pick[...], preferred_element_type=jnp.float32)
        for e in range(up.shape[0]):
            gate_pre = pre[:, 2 * e * units : (2 * e + 1) * units]
            up_pre = pre[:, (2 * e + 1) * units : (2 * e + 2) * units]
            value = gate_pre / (1.0 + jnp.exp(-gate_pre)) * up_pre * gates[:, e : e + 1]
            act[:, e * units : (e + 1) * units] = value.astype(jnp.bfloat16)

    @pl.when(step >= STEPS)
    def _():
        result = jnp.dot(act[...], down[...], preferred_element_type=jnp.float32).astype(
            jnp.bfloat16
        )
        at = 0
        for out in outs:
            out[...] = result[at : at + out.shape[0]]
            at += out.shape[0]


def run_experts(groups, up, down, pick):
    sizes = tuple(len(group) for group in groups)
    blocks = [block for group in groups for block in group]
    heights = [sum(block.shape[0] for block in group) for group in groups]
    height = sum(heights)
    experts, _, _, units = up.shape
    tile = D // STEPS
    early = lambda i: jnp.minimum(i, STEPS - 1)
    late = lambda i: jnp.maximum(i - STEPS, 0)
    return pl.pallas_call(
        functools.partial(experts_kernel, sizes),
        grid=(2 * STEPS,),
        in_specs=[pl.BlockSpec((b.shape[0], tile), lambda i: (0, early(i))) for b in blocks]
        + [pl.BlockSpec((b.shape[0], GATE_COLS), lambda i: (0, D // GATE_COLS)) for b in blocks]
        + [
            pl.BlockSpec((experts, 2, tile, units), lambda i: (0, 0, early(i), 0)),
            pl.BlockSpec((experts * units, tile), lambda i: (0, late(i))),
            pl.BlockSpec(pick.shape, lambda i: (0, 0)),
        ],
        out_specs=[pl.BlockSpec((h, tile), lambda i: (0, late(i))) for h in heights],
        out_shape=[jax.ShapeDtypeStruct((h, D), jnp.bfloat16) for h in heights],
        scratch_shapes=[
            pltpu.VMEM((height, experts * 2 * units), jnp.float32),
            pltpu.VMEM((height, experts * units), jnp.bfloat16),
        ],
        compiler_params=pltpu.CompilerParams(vmem_limit_bytes=40 * MIB),
        cost_estimate=pl.CostEstimate(
            flops=0, bytes_accessed=4096, transcendentals=0
        ),
    )(*blocks, *blocks, up, down, pick)


def document(positions, doc_ends):
    return jnp.sum((positions[:, None] >= doc_ends[None, :]).astype(jnp.int32), axis=1)


def attention(latent, query, w_uk, w_uv, doc_lengths):
    tokens = latent.shape[0]
    heads = w_uk.shape[0]
    qk_width = NOPE + ROPE
    score_scale = 1.0 / math.sqrt(qk_width)
    doc_ends = jnp.cumsum(doc_lengths)
    ctx = lax.axis_index("ctx")
    x_hi, y, core = ctx // 8, (ctx // 2) % 4, ctx % 2
    other = lax.ppermute(latent, BOTH, [(a, b) for a, b in table(dx=2) if a < b])
    blocks, places = [latent, other], [ctx, jnp.where(x_hi > 0, ctx - 8, NOWHERE)]
    for by in (1, -1, 2):
        to, come = (y + by) % 4, (y - by) % 4
        blocks.append(shift(jnp.where(to > y, latent, other), "y", by))
        place = x_hi * 8 + come * 2 + core
        places.append(
            jnp.where(come < y, place, jnp.where(x_hi > 0, place - 8, NOWHERE))
        )
    last = lax.ppermute(
        other,
        BOTH,
        [(a, b) for a, b in table(dy=1, dc=1) if a >= 64 and a // 8 % 2 and a // 16 % 4 < 3],
    )
    (half,) = stack(blocks)
    piece = jnp.concatenate([half, other_core(half), last], axis=0)
    starts = [place * tokens for place in places]
    starts += [(place + 1 - 2 * core) * tokens for place in places]
    seen = (x_hi > 0) & (core == 0) & (y > 0)
    starts.append(jnp.where(seen, ctx - 9, NOWHERE) * tokens)
    steps = jnp.arange(tokens, dtype=jnp.int32)
    key_pos = (jnp.stack(starts)[:, None] + steps[None, :]).reshape(-1)
    key_doc = document(key_pos, doc_ends)
    q_pos = ctx * tokens + steps
    q_doc = document(q_pos, doc_ends)
    q_rows = query.reshape(tokens, heads, qk_width)
    q_lat = jnp.einsum(
        "thn,hln->htl", q_rows[:, :, :NOPE], w_uk, preferred_element_type=jnp.float32
    ).astype(jnp.bfloat16)
    q_full = jnp.concatenate(
        [q_lat, jnp.transpose(q_rows[:, :, NOPE:], (1, 0, 2))], axis=2
    ).reshape(heads * tokens, LAT + ROPE)
    row_pos = jnp.tile(q_pos, heads)
    row_doc = jnp.tile(q_doc, heads)
    allowed = (row_doc[:, None] == key_doc[None, :]) & (row_pos[:, None] >= key_pos[None, :])
    scores = jnp.dot(q_full, piece.T, preferred_element_type=jnp.float32) * score_scale
    scores = jnp.where(allowed, scores, -1e30)
    row_max = jnp.max(scores, axis=1)
    weights = jnp.where(allowed, jnp.exp(scores - row_max[:, None]), 0.0)
    row_total = jnp.sum(weights, axis=1)
    accumulated = jnp.dot(
        weights.astype(jnp.bfloat16), piece[:, :LAT], preferred_element_type=jnp.float32
    )
    o_lat = (accumulated / row_total[:, None]).astype(jnp.bfloat16).reshape(heads, tokens, LAT)
    head_out = (
        jnp.einsum("htl,hlv->thv", o_lat, w_uv, preferred_element_type=jnp.float32)
        .astype(jnp.bfloat16)
        .reshape(tokens, heads * VDIM)
    )
    return head_out


def body(
    latent,
    query,
    w_uk,
    w_uv,
    w_o,
    residual,
    norm_gain,
    w_in,
    w_out,
    routes,
    gate_weights,
    doc_lengths,
):
    tokens = latent.shape[0]
    count_exp = lax.axis_size("exp")
    local_width = residual.shape[1]
    own = tokens // count_exp
    ctx, exp = lax.axis_index("ctx"), lax.axis_index("exp")
    local_experts = w_in.shape[0]
    units = w_in.shape[3]

    sent = jnp.concatenate(
        [
            residual.astype(jnp.float32).reshape(count_exp, own, local_width),
            jnp.broadcast_to(norm_gain[None, None, :], (count_exp, 1, local_width)),
        ],
        axis=1,
    )
    got = lax.all_to_all(sent, "exp", split_axis=0, concat_axis=0)
    wide = jnp.transpose(got, (1, 0, 2)).reshape(own + 1, D)
    residual_rows, gain = wide[:own], wide[own]

    own_routes = lax.dynamic_slice_in_dim(routes, exp * own, own, axis=0)
    own_gates = lax.dynamic_slice_in_dim(gate_weights, exp * own, own, axis=0)
    named = own_routes[:, :, None] == jnp.arange(EXPERTS, dtype=jnp.int32)[None, None, :]
    dense = jnp.sum(jnp.where(named, own_gates[:, :, None], 0.0), axis=1)
    high = dense.astype(jnp.bfloat16)
    low = (dense - high.astype(jnp.float32)).astype(jnp.bfloat16)
    gate_row = jnp.concatenate(
        [high, low, jnp.zeros((own, GATE_COLS - 2 * EXPERTS), jnp.bfloat16)], axis=1
    )
    column = jnp.arange(GATE_COLS, dtype=jnp.int32)[:, None]
    mine = ctx * local_experts + jnp.arange(local_experts, dtype=jnp.int32)[None, :]
    pick = ((column == mine) | (column == mine + EXPERTS)).astype(jnp.bfloat16)

    up = jnp.transpose(w_in, (0, 2, 1, 3))
    down = w_out.reshape(local_experts * units, D)

    def own_and_theirs(groups):
        theirs = [[other_core(block) for block in group] for group in groups]
        return run_experts(theirs + groups, up, down, pick)

    def both_cores(result):
        half = len(result) // 2
        return [
            add_up(here, other_core(there)).astype(jnp.bfloat16)
            for there, here in zip(result[:half], result[half:])
        ]

    head_out = attention(latent, query, w_uk, w_uv, doc_lengths)
    partial = jnp.dot(head_out, w_o, preferred_element_type=jnp.float32).astype(jnp.bfloat16)
    parts = lax.all_to_all(
        partial.reshape(count_exp, own, D), "exp", split_axis=0, concat_axis=0
    )
    parts, up = lax.optimization_barrier((parts, up))
    hidden = residual_rows + jnp.sum(parts.astype(jnp.float32), axis=0)
    squares = jnp.mean(hidden * hidden, axis=1, keepdims=True)
    normed = (hidden * lax.rsqrt(squares + epsilon) * gain[None, :]).astype(jnp.bfloat16)
    rows = jnp.concatenate([normed, gate_row], axis=1)

    x_own, x_before, x_after, x_far = ring(rows, "x")
    first, second = stack([x_own, x_before], [x_after, x_far])
    first, second = stack(ring(first, "z"), ring(second, "y"))
    near = first.shape[0] // 2
    before, after = [], []
    for block, axis in ((first, "y"), (second, "z")):
        before.append([shift(block, axis, 1)])
        after.append([shift(block, axis, -1)])
    at_own = own_and_theirs([[first], [second]])
    before, after, at_own = lax.optimization_barrier((before, after, at_own))
    far = []
    for i, axis in enumerate("yz"):
        far.append([shift(before[i][0][:near], axis, 1)])
        far.append([shift(after[i][0][near:], axis, -1)])
    at_before = own_and_theirs(before)
    far, at_before = lax.optimization_barrier((far, at_before))
    at_far = own_and_theirs(far)
    after, at_far = lax.optimization_barrier((after, at_far))
    sum_far = both_cores(at_far)
    passing = [
        (shift(sum_far[2 * i], axis, 1), shift(sum_far[2 * i + 1], axis, -1))
        for i, axis in enumerate("yz")
    ]
    passing, at_after = lax.optimization_barrier((passing, own_and_theirs(after)))
    back_own, back_before, back_after = [
        [other_core(there) for there in at[:2]] for at in (at_own, at_before, at_after)
    ]
    totals = []
    for i, axis in enumerate("yz"):
        for_after, for_before = passing[i]
        low = jnp.pad(for_before, ((near, 0), (0, 0)))
        high = jnp.pad(for_after, ((0, near), (0, 0)))
        sum_before = add_up(at_before[2 + i], back_before[i], low).astype(jnp.bfloat16)
        sum_after = add_up(at_after[2 + i], back_after[i], high).astype(jnp.bfloat16)
        totals.append(
            add_up(
                at_own[2 + i], back_own[i], shift(sum_before, axis, -1), shift(sum_after, axis, 1)
            ).astype(jnp.bfloat16)
        )
    first, second = totals
    pair = 2 * own
    first = ring_sum(*[first[i * pair : (i + 1) * pair] for i in range(4)], "z")
    second = ring_sum(*[second[i * pair : (i + 1) * pair] for i in range(4)], "y")
    first, second = first.astype(jnp.bfloat16), second.astype(jnp.bfloat16)
    moe_out = ring_sum(first[:own], first[own:], second[:own], second[own:], "x")
    mixed = (hidden + moe_out).astype(jnp.bfloat16)
    return lax.all_to_all(mixed, "exp", split_axis=1, concat_axis=0, tiled=True)


def solution(mesh):
    placed = (
        P("ctx", None),
        P("ctx", "exp"),
        P("exp", None, None),
        P("exp", None, None),
        P("exp", None),
        P("ctx", "exp"),
        P("exp"),
        P("ctx", None, None, "exp"),
        P("ctx", "exp", None),
        P("ctx", None),
        P("ctx", None),
        P(),
    )
    return jax.shard_map(
        body, mesh=mesh, in_specs=placed, out_specs=P("ctx", "exp"), check_vma=False
    )
```

```python
import functools
import itertools
import math

import jax
import jax.numpy as jnp
from jax import lax
from jax.experimental import pallas as pl
from jax.experimental.pallas import tpu as pltpu
from jax.sharding import PartitionSpec as P

D = 4096
NOPE = 128
ROPE = 64
LAT = 512
VDIM = 128
TOP = 8
EXPERTS = 32
GATE_COLS = 128
BOTH = ("ctx", "exp")
NOWHERE = 64

epsilon = 1e-06


def table(dx=0, dy=0, dz=0, dc=0):
    def at(x, y, z, c):
        return ((x // 2 * 4 + y) * 2 + c) * 8 + z * 2 + x % 2

    return [
        (at(x, y, z, c), at((x + dx) % 4, (y + dy) % 4, (z + dz) % 4, (c + dc) % 2))
        for x, y, z, c in itertools.product(range(4), range(4), range(4), range(2))
    ]


def shift(value, axis, by):
    return lax.ppermute(value, BOTH, table(**{"d" + axis: by}))


def other_core(value):
    return shift(value, "c", 1)


def ring(block, axis):
    return [block, shift(block, axis, 1), shift(block, axis, -1), shift(block, axis, 2)]


def add_up(*blocks):
    total = blocks[0].astype(jnp.float32)
    for block in blocks[1:]:
        total = total + block.astype(jnp.float32)
    return total


def ring_sum(own, before, after, far, axis):
    return add_up(own, shift(before, axis, -1), shift(after, axis, 1), shift(far, axis, 2))


MIB = 1024 * 1024


def grouped(refs, sizes):
    found, at = [], 0
    for size in sizes:
        found.append(refs[at : at + size])
        at += size
    return found


def stack_kernel(sizes, *refs):
    count = sum(sizes)
    for group, out in zip(grouped(refs[:count], sizes), refs[count:]):
        at = 0
        for ref in group:
            out[at : at + ref.shape[0], :] = ref[...]
            at += ref.shape[0]


def stack(*groups):
    sizes = tuple(len(group) for group in groups)
    blocks = [block for group in groups for block in group]
    width = blocks[0].shape[1]
    heights = [sum(block.shape[0] for block in group) for group in groups]
    cuts = 3 if width % 384 == 0 else 1
    tile = width // cuts
    return pl.pallas_call(
        functools.partial(stack_kernel, sizes),
        grid=(cuts,),
        in_specs=[pl.BlockSpec((block.shape[0], tile), lambda i: (0, i)) for block in blocks],
        out_specs=[pl.BlockSpec((height, tile), lambda i: (0, i)) for height in heights],
        out_shape=[jax.ShapeDtypeStruct((height, width), jnp.bfloat16) for height in heights],
        compiler_params=pltpu.CompilerParams(vmem_limit_bytes=16 * MIB),
        cost_estimate=pl.CostEstimate(
            flops=0, bytes_accessed=4 * sum(heights) * width, transcendentals=0
        ),
    )(*blocks)


STEPS = 2


def experts_kernel(sizes, *refs):
    count = sum(sizes)
    blocks, gate_refs = refs[:count], refs[count : 2 * count]
    up, down, pick = refs[2 * count : 2 * count + 3]
    outs = refs[2 * count + 3 : 2 * count + 3 + len(sizes)]
    pre, act = refs[2 * count + 3 + len(sizes) :]
    step = pl.program_id(0)
    units = up.shape[3]

    @pl.when(step == 0)
    def _():
        pre[...] = jnp.zeros_like(pre)

    @pl.when(step < STEPS)
    def _():
        rows = jnp.concatenate([block[...] for block in blocks], axis=0)
        weights = jnp.concatenate(
            [up[e, g] for e in range(up.shape[0]) for g in range(2)], axis=1
        )
        pre[...] += jnp.dot(rows, weights, preferred_element_type=jnp.float32)

    @pl.when(step == STEPS - 1)
    def _():
        gate_rows = jnp.concatenate([ref[...] for ref in gate_refs], axis=0)
        gates = jnp.dot(gate_rows, pick[...], preferred_element_type=jnp.float32)
        for e in range(up.shape[0]):
            gate_pre = pre[:, 2 * e * units : (2 * e + 1) * units]
            up_pre = pre[:, (2 * e + 1) * units : (2 * e + 2) * units]
            value = gate_pre / (1.0 + jnp.exp(-gate_pre)) * up_pre * gates[:, e : e + 1]
            act[:, e * units : (e + 1) * units] = value.astype(jnp.bfloat16)

    @pl.when(step >= STEPS)
    def _():
        result = jnp.dot(act[...], down[...], preferred_element_type=jnp.float32).astype(
            jnp.bfloat16
        )
        at = 0
        for out in outs:
            out[...] = result[at : at + out.shape[0]]
            at += out.shape[0]


def run_experts(groups, up, down, pick):
    sizes = tuple(len(group) for group in groups)
    blocks = [block for group in groups for block in group]
    heights = [sum(block.shape[0] for block in group) for group in groups]
    height = sum(heights)
    experts, _, _, units = up.shape
    tile = D // STEPS
    early = lambda i: jnp.minimum(i, STEPS - 1)
    late = lambda i: jnp.maximum(i - STEPS, 0)
    return pl.pallas_call(
        functools.partial(experts_kernel, sizes),
        grid=(2 * STEPS,),
        in_specs=[pl.BlockSpec((b.shape[0], tile), lambda i: (0, early(i))) for b in blocks]
        + [pl.BlockSpec((b.shape[0], GATE_COLS), lambda i: (0, D // GATE_COLS)) for b in blocks]
        + [
            pl.BlockSpec((experts, 2, tile, units), lambda i: (0, 0, early(i), 0)),
            pl.BlockSpec((experts * units, tile), lambda i: (0, late(i))),
            pl.BlockSpec(pick.shape, lambda i: (0, 0)),
        ],
        out_specs=[pl.BlockSpec((h, tile), lambda i: (0, late(i))) for h in heights],
        out_shape=[jax.ShapeDtypeStruct((h, D), jnp.bfloat16) for h in heights],
        scratch_shapes=[
            pltpu.VMEM((height, experts * 2 * units), jnp.float32),
            pltpu.VMEM((height, experts * units), jnp.bfloat16),
        ],
        compiler_params=pltpu.CompilerParams(vmem_limit_bytes=40 * MIB),
        cost_estimate=pl.CostEstimate(
            flops=0, bytes_accessed=4096, transcendentals=0
        ),
    )(*blocks, *blocks, up, down, pick)


def document(positions, doc_ends):
    return jnp.sum((positions[:, None] >= doc_ends[None, :]).astype(jnp.int32), axis=1)


def attention(latent, query, w_uk, w_uv, doc_lengths, sent):
    tokens = latent.shape[0]
    heads = w_uk.shape[0]
    qk_width = NOPE + ROPE
    score_scale = 1.0 / math.sqrt(qk_width)
    doc_ends = jnp.cumsum(doc_lengths)
    ctx = lax.axis_index("ctx")
    x_hi, y, core = ctx // 8, (ctx // 2) % 4, ctx % 2
    other = lax.ppermute(latent, BOTH, [(a, b) for a, b in table(dx=2) if a < b])
    blocks, places = [latent, other], [ctx, jnp.where(x_hi > 0, ctx - 8, NOWHERE)]
    for by in (1, -1, 2):
        to, come = (y + by) % 4, (y - by) % 4
        blocks.append(shift(jnp.where(to > y, latent, other), "y", by))
        place = x_hi * 8 + come * 2 + core
        places.append(
            jnp.where(come < y, place, jnp.where(x_hi > 0, place - 8, NOWHERE))
        )
    last = lax.ppermute(
        other,
        BOTH,
        [(a, b) for a, b in table(dy=1, dc=1) if a >= 64 and a // 8 % 2 and a // 16 % 4 < 3],
    )
    (half,) = stack(blocks)
    half, sent = lax.optimization_barrier((half, sent))
    (piece,) = stack([half, other_core(half), last])
    starts = [place * tokens for place in places]
    starts += [(place + 1 - 2 * core) * tokens for place in places]
    seen = (x_hi > 0) & (core == 0) & (y > 0)
    starts.append(jnp.where(seen, ctx - 9, NOWHERE) * tokens)
    steps = jnp.arange(tokens, dtype=jnp.int32)
    key_pos = (jnp.stack(starts)[:, None] + steps[None, :]).reshape(-1)
    key_doc = document(key_pos, doc_ends)
    q_pos = ctx * tokens + steps
    q_doc = document(q_pos, doc_ends)
    q_rows = query.reshape(tokens, heads, qk_width)
    q_lat = jnp.einsum(
        "thn,hln->htl", q_rows[:, :, :NOPE], w_uk, preferred_element_type=jnp.float32
    ).astype(jnp.bfloat16)
    q_full = jnp.concatenate(
        [q_lat, jnp.transpose(q_rows[:, :, NOPE:], (1, 0, 2))], axis=2
    ).reshape(heads * tokens, LAT + ROPE)
    row_pos = jnp.tile(q_pos, heads)
    row_doc = jnp.tile(q_doc, heads)
    allowed = (row_doc[:, None] == key_doc[None, :]) & (row_pos[:, None] >= key_pos[None, :])
    scores = jnp.dot(q_full, piece.T, preferred_element_type=jnp.float32) * score_scale
    scores = jnp.where(allowed, scores, -1e30)
    row_max = jnp.max(scores, axis=1)
    weights = jnp.where(allowed, jnp.exp(scores - row_max[:, None]), 0.0)
    row_total = jnp.sum(weights, axis=1)
    accumulated = jnp.dot(
        weights.astype(jnp.bfloat16), piece[:, :LAT], preferred_element_type=jnp.float32
    )
    o_lat = (accumulated / row_total[:, None]).astype(jnp.bfloat16).reshape(heads, tokens, LAT)
    head_out = (
        jnp.einsum("htl,hlv->thv", o_lat, w_uv, preferred_element_type=jnp.float32)
        .astype(jnp.bfloat16)
        .reshape(tokens, heads * VDIM)
    )
    return head_out, sent


def body(
    latent,
    query,
    w_uk,
    w_uv,
    w_o,
    residual,
    norm_gain,
    w_in,
    w_out,
    routes,
    gate_weights,
    doc_lengths,
):
    tokens = latent.shape[0]
    count_exp = lax.axis_size("exp")
    local_width = residual.shape[1]
    own = tokens // count_exp
    ctx, exp = lax.axis_index("ctx"), lax.axis_index("exp")
    local_experts = w_in.shape[0]
    units = w_in.shape[3]

    sent = jnp.concatenate(
        [
            residual.astype(jnp.float32).reshape(count_exp, own, local_width),
            jnp.broadcast_to(norm_gain[None, None, :], (count_exp, 1, local_width)),
        ],
        axis=1,
    )
    own_routes = lax.dynamic_slice_in_dim(routes, exp * own, own, axis=0)
    own_gates = lax.dynamic_slice_in_dim(gate_weights, exp * own, own, axis=0)
    named = own_routes[:, :, None] == jnp.arange(EXPERTS, dtype=jnp.int32)[None, None, :]
    dense = jnp.sum(jnp.where(named, own_gates[:, :, None], 0.0), axis=1)
    high = dense.astype(jnp.bfloat16)
    low = (dense - high.astype(jnp.float32)).astype(jnp.bfloat16)
    gate_row = jnp.concatenate(
        [high, low, jnp.zeros((own, GATE_COLS - 2 * EXPERTS), jnp.bfloat16)], axis=1
    )
    column = jnp.arange(GATE_COLS, dtype=jnp.int32)[:, None]
    mine = ctx * local_experts + jnp.arange(local_experts, dtype=jnp.int32)[None, :]
    pick = ((column == mine) | (column == mine + EXPERTS)).astype(jnp.bfloat16)

    up = jnp.transpose(w_in, (0, 2, 1, 3))
    down = w_out.reshape(local_experts * units, D)

    def both_cores(blocks):
        theirs = [other_core(block) for block in blocks]
        result = run_experts([theirs] + [[block] for block in blocks], up, down, pick)
        return result[1:], result[0]

    def summed(result, extra=None):
        here, there = result
        back = other_core(there)
        rows = here[0].shape[0]
        return [
            add_up(
                block,
                back[i * rows : (i + 1) * rows],
                *(() if extra is None else (extra[i],)),
            ).astype(jnp.bfloat16)
            for i, block in enumerate(here)
        ]

    head_out, sent = attention(latent, query, w_uk, w_uv, doc_lengths, sent)
    got = lax.all_to_all(sent, "exp", split_axis=0, concat_axis=0)
    wide = jnp.transpose(got, (1, 0, 2)).reshape(own + 1, D)
    residual_rows, gain = wide[:own], wide[own]
    partial = jnp.dot(head_out, w_o, preferred_element_type=jnp.float32).astype(jnp.bfloat16)
    parts = lax.all_to_all(
        partial.reshape(count_exp, own, D), "exp", split_axis=0, concat_axis=0
    )
    parts, up = lax.optimization_barrier((parts, up))
    hidden = residual_rows + jnp.sum(parts.astype(jnp.float32), axis=0)
    squares = jnp.mean(hidden * hidden, axis=1, keepdims=True)
    normed = (hidden * lax.rsqrt(squares + epsilon) * gain[None, :]).astype(jnp.bfloat16)
    rows = jnp.concatenate([normed, gate_row], axis=1)

    x_own, x_before, x_after, x_far = ring(rows, "x")
    first, second = stack([x_own, x_before], [x_after, x_far])
    by_z, by_y = ring(first, "z"), ring(second, "y")
    halves = stack(by_z[:2], by_z[2:], by_y[:2], by_y[2:])
    y_low, y_high, z_low, z_high = halves

    def near(low, high, axis):
        return [shift(low, axis, 1), shift(high, axis, -1)]

    near_a = near(y_low, y_high, "y") + near(z_low, z_high, "z")
    near_a, at_own = lax.optimization_barrier((near_a, both_cores(halves)))
    far = near(*near_a[:2], "y") + near(*near_a[2:], "z")
    far, at_a = lax.optimization_barrier((far, both_cores(near_a)))
    halves, far = lax.optimization_barrier((halves, far))
    y_low, y_high, z_low, z_high = halves
    near_b = near(y_high, y_low, "y") + near(z_high, z_low, "z")
    near_b, at_far = lax.optimization_barrier((near_b, both_cores(far)))
    sum_far = summed(at_far)
    passing = near(*sum_far[:2], "y") + near(*sum_far[2:], "z")
    passing, at_b = lax.optimization_barrier((passing, both_cores(near_b)))
    sum_a = summed(at_a)
    back_a = near(sum_a[1], sum_a[0], "y") + near(sum_a[3], sum_a[2], "z")
    sum_b = summed(at_b, [passing[1], passing[0], passing[3], passing[2]])
    back_b = near(sum_b[1], sum_b[0], "y") + near(sum_b[3], sum_b[2], "z")
    own_here, own_there = at_own
    own_back = other_core(own_there)
    rows = 4 * own
    pair = 2 * own

    def final(i, k, *arrived):
        part = slice(k * pair, (k + 1) * pair)
        return add_up(
            own_here[i][part],
            own_back[i * rows : (i + 1) * rows][part],
            *[block[part] for block in arrived],
        ).astype(jnp.bfloat16)

    sums = []
    for i in range(4):
        at = i // 2 * 2
        if i % 2 == 0:
            arrived = (back_a[at + 1], back_b[at])
        else:
            arrived = (back_a[at], back_b[at + 1])
        sums += [final(i, k, *arrived) for k in range(2)]
    first = ring_sum(*sums[:4], "z").astype(jnp.bfloat16)
    second = ring_sum(*sums[4:], "y").astype(jnp.bfloat16)
    moe_out = ring_sum(first[:own], first[own:], second[:own], second[own:], "x")
    mixed = (hidden + moe_out).astype(jnp.bfloat16)
    return lax.all_to_all(mixed, "exp", split_axis=1, concat_axis=0, tiled=True)


def solution(mesh):
    placed = (
        P("ctx", None),
        P("ctx", "exp"),
        P("exp", None, None),
        P("exp", None, None),
        P("exp", None),
        P("ctx", "exp"),
        P("exp"),
        P("ctx", None, None, "exp"),
        P("ctx", "exp", None),
        P("ctx", None),
        P("ctx", None),
        P(),
    )
    return jax.shard_map(
        body, mesh=mesh, in_specs=placed, out_specs=P("ctx", "exp"), check_vma=False
    )
```

```python
import functools
import itertools
import math

import jax
import jax.numpy as jnp
from jax import lax
from jax.experimental import pallas as pl
from jax.experimental.pallas import tpu as pltpu
from jax.sharding import PartitionSpec as P

D = 4096
NOPE = 128
ROPE = 64
LAT = 512
VDIM = 128
TOP = 8
EXPERTS = 32
GATE_COLS = 128
BOTH = ("ctx", "exp")
NOWHERE = 64

epsilon = 1e-06


def table(dx=0, dy=0, dz=0, dc=0):
    def at(x, y, z, c):
        return ((x // 2 * 4 + y) * 2 + c) * 8 + z * 2 + x % 2

    return [
        (at(x, y, z, c), at((x + dx) % 4, (y + dy) % 4, (z + dz) % 4, (c + dc) % 2))
        for x, y, z, c in itertools.product(range(4), range(4), range(4), range(2))
    ]


def row(device):
    return device // 16 % 4


def shift(value, axis, by):
    return lax.ppermute(value, BOTH, table(**{"d" + axis: by}))


def other_core(value):
    return shift(value, "c", 1)


def ring(block, axis):
    return [block, shift(block, axis, 1), shift(block, axis, -1), shift(block, axis, 2)]


def add_up(*blocks):
    total = blocks[0].astype(jnp.float32)
    for block in blocks[1:]:
        total = total + block.astype(jnp.float32)
    return total


def ring_sum(own, before, after, far, axis):
    return add_up(own, shift(before, axis, -1), shift(after, axis, 1), shift(far, axis, 2))


MIB = 1024 * 1024


def grouped(refs, sizes):
    found, at = [], 0
    for size in sizes:
        found.append(refs[at : at + size])
        at += size
    return found


def stack_kernel(sizes, *refs):
    count = sum(sizes)
    for group, out in zip(grouped(refs[:count], sizes), refs[count:]):
        at = 0
        for ref in group:
            out[at : at + ref.shape[0], :] = ref[...]
            at += ref.shape[0]


def stack(*groups):
    sizes = tuple(len(group) for group in groups)
    blocks = [block for group in groups for block in group]
    width = blocks[0].shape[1]
    heights = [sum(block.shape[0] for block in group) for group in groups]
    cuts = 3 if width % 384 == 0 else 1
    tile = width // cuts
    return pl.pallas_call(
        functools.partial(stack_kernel, sizes),
        grid=(cuts,),
        in_specs=[pl.BlockSpec((block.shape[0], tile), lambda i: (0, i)) for block in blocks],
        out_specs=[pl.BlockSpec((height, tile), lambda i: (0, i)) for height in heights],
        out_shape=[jax.ShapeDtypeStruct((height, width), jnp.bfloat16) for height in heights],
        compiler_params=pltpu.CompilerParams(vmem_limit_bytes=16 * MIB),
        cost_estimate=pl.CostEstimate(
            flops=0, bytes_accessed=4 * sum(heights) * width, transcendentals=0
        ),
    )(*blocks)


STEPS = 2


def experts_kernel(sizes, *refs):
    count = sum(sizes)
    blocks, gate_refs = refs[:count], refs[count : 2 * count]
    up, down, pick = refs[2 * count : 2 * count + 3]
    outs = refs[2 * count + 3 : 2 * count + 3 + len(sizes)]
    pre, act = refs[2 * count + 3 + len(sizes) :]
    step = pl.program_id(0)
    units = up.shape[3]

    @pl.when(step == 0)
    def _():
        pre[...] = jnp.zeros_like(pre)

    @pl.when(step < STEPS)
    def _():
        rows = jnp.concatenate([block[...] for block in blocks], axis=0)
        weights = jnp.concatenate(
            [up[e, g] for e in range(up.shape[0]) for g in range(2)], axis=1
        )
        pre[...] += jnp.dot(rows, weights, preferred_element_type=jnp.float32)

    @pl.when(step == STEPS - 1)
    def _():
        gate_rows = jnp.concatenate([ref[...] for ref in gate_refs], axis=0)
        gates = jnp.dot(gate_rows, pick[...], preferred_element_type=jnp.float32)
        for e in range(up.shape[0]):
            gate_pre = pre[:, 2 * e * units : (2 * e + 1) * units]
            up_pre = pre[:, (2 * e + 1) * units : (2 * e + 2) * units]
            value = gate_pre / (1.0 + jnp.exp(-gate_pre)) * up_pre * gates[:, e : e + 1]
            act[:, e * units : (e + 1) * units] = value.astype(jnp.bfloat16)

    @pl.when(step >= STEPS)
    def _():
        result = jnp.dot(act[...], down[...], preferred_element_type=jnp.float32).astype(
            jnp.bfloat16
        )
        at = 0
        for out in outs:
            out[...] = result[at : at + out.shape[0]]
            at += out.shape[0]


def run_experts(groups, up, down, pick):
    sizes = tuple(len(group) for group in groups)
    blocks = [block for group in groups for block in group]
    heights = [sum(block.shape[0] for block in group) for group in groups]
    height = sum(heights)
    experts, _, _, units = up.shape
    tile = D // STEPS
    early = lambda i: jnp.minimum(i, STEPS - 1)
    late = lambda i: jnp.maximum(i - STEPS, 0)
    return pl.pallas_call(
        functools.partial(experts_kernel, sizes),
        grid=(2 * STEPS,),
        in_specs=[pl.BlockSpec((b.shape[0], tile), lambda i: (0, early(i))) for b in blocks]
        + [pl.BlockSpec((b.shape[0], GATE_COLS), lambda i: (0, D // GATE_COLS)) for b in blocks]
        + [
            pl.BlockSpec((experts, 2, tile, units), lambda i: (0, 0, early(i), 0)),
            pl.BlockSpec((experts * units, tile), lambda i: (0, late(i))),
            pl.BlockSpec(pick.shape, lambda i: (0, 0)),
        ],
        out_specs=[pl.BlockSpec((h, tile), lambda i: (0, late(i))) for h in heights],
        out_shape=[jax.ShapeDtypeStruct((h, D), jnp.bfloat16) for h in heights],
        scratch_shapes=[
            pltpu.VMEM((height, experts * 2 * units), jnp.float32),
            pltpu.VMEM((height, experts * units), jnp.bfloat16),
        ],
        compiler_params=pltpu.CompilerParams(vmem_limit_bytes=40 * MIB),
        cost_estimate=pl.CostEstimate(
            flops=0, bytes_accessed=4096, transcendentals=0
        ),
    )(*blocks, *blocks, up, down, pick)


def document(positions, doc_ends):
    return jnp.sum((positions[:, None] >= doc_ends[None, :]).astype(jnp.int32), axis=1)


def attention(latent, query, w_uk, w_uv, doc_lengths):
    tokens = latent.shape[0]
    heads = w_uk.shape[0]
    qk_width = NOPE + ROPE
    score_scale = 1.0 / math.sqrt(qk_width)
    doc_ends = jnp.cumsum(doc_lengths)
    ctx = lax.axis_index("ctx")
    x_hi, y, core = ctx // 8, (ctx // 2) % 4, ctx % 2
    blocks, places = [latent], [ctx]
    for by in (0, 1, -1, 2):
        come = (y - by) % 4
        same = [(a, b) for a, b in table(dy=by) if row(a) < row(b)]
        across = [(a, b) for a, b in table(dx=2, dy=by) if a < 64 and row(a) >= row(b)]
        blocks.append(lax.ppermute(latent, BOTH, same + across))
        place = x_hi * 8 + come * 2 + core
        places.append(
            jnp.where(come < y, place, jnp.where(x_hi > 0, place - 8, NOWHERE))
        )
    last = lax.ppermute(
        latent,
        BOTH,
        [(a, b) for a, b in table(dx=2, dy=1, dc=1) if a < 64 and a // 8 % 2 and row(a) < 3],
    )
    (half,) = stack(blocks)
    (piece,) = stack([half, other_core(half), last])
    starts = [place * tokens for place in places]
    starts += [(place + 1 - 2 * core) * tokens for place in places]
    seen = (x_hi > 0) & (core == 0) & (y > 0)
    starts.append(jnp.where(seen, ctx - 9, NOWHERE) * tokens)
    steps = jnp.arange(tokens, dtype=jnp.int32)
    key_pos = (jnp.stack(starts)[:, None] + steps[None, :]).reshape(-1)
    key_doc = document(key_pos, doc_ends)
    q_pos = ctx * tokens + steps
    q_doc = document(q_pos, doc_ends)
    q_rows = query.reshape(tokens, heads, qk_width)
    q_lat = jnp.einsum(
        "thn,hln->htl", q_rows[:, :, :NOPE], w_uk, preferred_element_type=jnp.float32
    ).astype(jnp.bfloat16)
    q_full = jnp.concatenate(
        [q_lat, jnp.transpose(q_rows[:, :, NOPE:], (1, 0, 2))], axis=2
    ).reshape(heads * tokens, LAT + ROPE)
    row_pos = jnp.tile(q_pos, heads)
    row_doc = jnp.tile(q_doc, heads)
    allowed = (row_doc[:, None] == key_doc[None, :]) & (row_pos[:, None] >= key_pos[None, :])
    scores = jnp.dot(q_full, piece.T, preferred_element_type=jnp.float32) * score_scale
    scores = jnp.where(allowed, scores, -1e30)
    row_max = jnp.max(scores, axis=1)
    weights = jnp.where(allowed, jnp.exp(scores - row_max[:, None]), 0.0)
    row_total = jnp.sum(weights, axis=1)
    accumulated = jnp.dot(
        weights.astype(jnp.bfloat16), piece[:, :LAT], preferred_element_type=jnp.float32
    )
    o_lat = (accumulated / row_total[:, None]).astype(jnp.bfloat16).reshape(heads, tokens, LAT)
    head_out = (
        jnp.einsum("htl,hlv->thv", o_lat, w_uv, preferred_element_type=jnp.float32)
        .astype(jnp.bfloat16)
        .reshape(tokens, heads * VDIM)
    )
    return head_out


def body(
    latent,
    query,
    w_uk,
    w_uv,
    w_o,
    residual,
    norm_gain,
    w_in,
    w_out,
    routes,
    gate_weights,
    doc_lengths,
):
    tokens = latent.shape[0]
    count_exp = lax.axis_size("exp")
    local_width = residual.shape[1]
    own = tokens // count_exp
    ctx, exp = lax.axis_index("ctx"), lax.axis_index("exp")
    local_experts = w_in.shape[0]
    units = w_in.shape[3]

    sent = jnp.concatenate(
        [
            residual.astype(jnp.float32).reshape(count_exp, own, local_width),
            jnp.broadcast_to(norm_gain[None, None, :], (count_exp, 1, local_width)),
        ],
        axis=1,
    )
    own_routes = lax.dynamic_slice_in_dim(routes, exp * own, own, axis=0)
    own_gates = lax.dynamic_slice_in_dim(gate_weights, exp * own, own, axis=0)
    named = own_routes[:, :, None] == jnp.arange(EXPERTS, dtype=jnp.int32)[None, None, :]
    dense = jnp.sum(jnp.where(named, own_gates[:, :, None], 0.0), axis=1)
    high = dense.astype(jnp.bfloat16)
    low = (dense - high.astype(jnp.float32)).astype(jnp.bfloat16)
    gate_row = jnp.concatenate(
        [high, low, jnp.zeros((own, GATE_COLS - 2 * EXPERTS), jnp.bfloat16)], axis=1
    )
    column = jnp.arange(GATE_COLS, dtype=jnp.int32)[:, None]
    mine = ctx * local_experts + jnp.arange(local_experts, dtype=jnp.int32)[None, :]
    pick = ((column == mine) | (column == mine + EXPERTS)).astype(jnp.bfloat16)

    up = jnp.transpose(w_in, (0, 2, 1, 3))
    down = w_out.reshape(local_experts * units, D)

    def both_cores(blocks):
        theirs = [other_core(block) for block in blocks]
        result = run_experts([theirs] + [[block] for block in blocks], up, down, pick)
        return result[1:], result[0]

    def summed(result, extra=None):
        here, there = result
        back = other_core(there)
        rows = here[0].shape[0]
        return [
            add_up(
                block,
                back[i * rows : (i + 1) * rows],
                *(() if extra is None else (extra[i],)),
            ).astype(jnp.bfloat16)
            for i, block in enumerate(here)
        ]

    head_out = attention(latent, query, w_uk, w_uv, doc_lengths)
    got = lax.all_to_all(sent, "exp", split_axis=0, concat_axis=0)
    wide = jnp.transpose(got, (1, 0, 2)).reshape(own + 1, D)
    residual_rows, gain = wide[:own], wide[own]
    partial = jnp.dot(head_out, w_o, preferred_element_type=jnp.float32).astype(jnp.bfloat16)
    parts = lax.all_to_all(
        partial.reshape(count_exp, own, D), "exp", split_axis=0, concat_axis=0
    )
    parts, up = lax.optimization_barrier((parts, up))
    hidden = residual_rows + jnp.sum(parts.astype(jnp.float32), axis=0)
    squares = jnp.mean(hidden * hidden, axis=1, keepdims=True)
    normed = (hidden * lax.rsqrt(squares + epsilon) * gain[None, :]).astype(jnp.bfloat16)
    rows = jnp.concatenate([normed, gate_row], axis=1)

    x_own, x_before, x_after, x_far = ring(rows, "x")
    first, second = stack([x_own, x_before], [x_after, x_far])
    by_z, by_y = ring(first, "z"), ring(second, "y")
    halves = stack(by_z[:2], by_z[2:], by_y[:2], by_y[2:])
    y_low, y_high, z_low, z_high = halves

    def near(low, high, axis):
        return [shift(low, axis, 1), shift(high, axis, -1)]

    near_a = near(y_low, y_high, "y") + near(z_low, z_high, "z")
    near_a, at_own = lax.optimization_barrier((near_a, both_cores(halves)))
    far = near(*near_a[:2], "y") + near(*near_a[2:], "z")
    far, at_a = lax.optimization_barrier((far, both_cores(near_a)))
    halves, far = lax.optimization_barrier((halves, far))
    y_low, y_high, z_low, z_high = halves
    near_b = near(y_high, y_low, "y") + near(z_high, z_low, "z")
    near_b, at_far = lax.optimization_barrier((near_b, both_cores(far)))
    sum_far = summed(at_far)
    sum_a = summed(at_a)
    back_a = near(sum_a[1], sum_a[0], "y") + near(sum_a[3], sum_a[2], "z")
    back_a, at_b = lax.optimization_barrier((back_a, both_cores(near_b)))
    passing = near(*sum_far[:2], "y") + near(*sum_far[2:], "z")
    sum_b = summed(at_b, [passing[1], passing[0], passing[3], passing[2]])
    back_b = near(sum_b[1], sum_b[0], "y") + near(sum_b[3], sum_b[2], "z")
    own_here, own_there = at_own
    own_back = other_core(own_there)
    rows = 4 * own
    pair = 2 * own

    def final(i, k, *arrived):
        part = slice(k * pair, (k + 1) * pair)
        return add_up(
            own_here[i][part],
            own_back[i * rows : (i + 1) * rows][part],
            *[block[part] for block in arrived],
        ).astype(jnp.bfloat16)

    sums = []
    for i in range(4):
        at = i // 2 * 2
        if i % 2 == 0:
            arrived = (back_a[at + 1], back_b[at])
        else:
            arrived = (back_a[at], back_b[at + 1])
        sums += [final(i, k, *arrived) for k in range(2)]
    first = ring_sum(*sums[:4], "z").astype(jnp.bfloat16)
    second = ring_sum(*sums[4:], "y").astype(jnp.bfloat16)
    moe_out = ring_sum(first[:own], first[own:], second[:own], second[own:], "x")
    mixed = (hidden + moe_out).astype(jnp.bfloat16)
    return lax.all_to_all(mixed, "exp", split_axis=1, concat_axis=0, tiled=True)


def solution(mesh):
    placed = (
        P("ctx", None),
        P("ctx", "exp"),
        P("exp", None, None),
        P("exp", None, None),
        P("exp", None),
        P("ctx", "exp"),
        P("exp"),
        P("ctx", None, None, "exp"),
        P("ctx", "exp", None),
        P("ctx", None),
        P("ctx", None),
        P(),
    )
    return jax.shard_map(
        body, mesh=mesh, in_specs=placed, out_specs=P("ctx", "exp"), check_vma=False
    )
```

```python
import functools
import itertools
import math

import jax
import jax.numpy as jnp
from jax import lax
from jax.experimental import pallas as pl
from jax.experimental.pallas import tpu as pltpu
from jax.sharding import PartitionSpec as P

D = 4096
NOPE = 128
ROPE = 64
LAT = 512
VDIM = 128
TOP = 8
EXPERTS = 32
GATE_COLS = 128
BOTH = ("ctx", "exp")
NOWHERE = 64

epsilon = 1e-06


def table(dx=0, dy=0, dz=0, dc=0):
    def at(x, y, z, c):
        return ((x // 2 * 4 + y) * 2 + c) * 8 + z * 2 + x % 2

    return [
        (at(x, y, z, c), at((x + dx) % 4, (y + dy) % 4, (z + dz) % 4, (c + dc) % 2))
        for x, y, z, c in itertools.product(range(4), range(4), range(4), range(2))
    ]


def row(device):
    return device // 16 % 4


def shift(value, axis, by):
    return lax.ppermute(value, BOTH, table(**{"d" + axis: by}))


def other_core(value):
    return shift(value, "c", 1)


def ring(block, axis):
    return [block, shift(block, axis, 1), shift(block, axis, -1), shift(block, axis, 2)]


def add_up(*blocks):
    total = blocks[0].astype(jnp.float32)
    for block in blocks[1:]:
        total = total + block.astype(jnp.float32)
    return total


def ring_sum(own, before, after, far, axis):
    return add_up(own, shift(before, axis, -1), shift(after, axis, 1), shift(far, axis, 2))


MIB = 1024 * 1024


def grouped(refs, sizes):
    found, at = [], 0
    for size in sizes:
        found.append(refs[at : at + size])
        at += size
    return found


def stack_kernel(sizes, *refs):
    count = sum(sizes)
    for group, out in zip(grouped(refs[:count], sizes), refs[count:]):
        at = 0
        for ref in group:
            out[at : at + ref.shape[0], :] = ref[...]
            at += ref.shape[0]


def stack(*groups):
    sizes = tuple(len(group) for group in groups)
    blocks = [block for group in groups for block in group]
    width = blocks[0].shape[1]
    heights = [sum(block.shape[0] for block in group) for group in groups]
    cuts = 3 if width % 384 == 0 else 1
    tile = width // cuts
    return pl.pallas_call(
        functools.partial(stack_kernel, sizes),
        grid=(cuts,),
        in_specs=[pl.BlockSpec((block.shape[0], tile), lambda i: (0, i)) for block in blocks],
        out_specs=[pl.BlockSpec((height, tile), lambda i: (0, i)) for height in heights],
        out_shape=[jax.ShapeDtypeStruct((height, width), jnp.bfloat16) for height in heights],
        compiler_params=pltpu.CompilerParams(vmem_limit_bytes=16 * MIB),
        cost_estimate=pl.CostEstimate(
            flops=0, bytes_accessed=4 * sum(heights) * width, transcendentals=0
        ),
    )(*blocks)


STEPS = 2


def experts_kernel(sizes, *refs):
    count = sum(sizes)
    blocks, gate_refs = refs[:count], refs[count : 2 * count]
    up, down, pick = refs[2 * count : 2 * count + 3]
    outs = refs[2 * count + 3 : 2 * count + 3 + len(sizes)]
    pre, act = refs[2 * count + 3 + len(sizes) :]
    step = pl.program_id(0)
    units = up.shape[3]

    @pl.when(step == 0)
    def _():
        pre[...] = jnp.zeros_like(pre)

    @pl.when(step < STEPS)
    def _():
        rows = jnp.concatenate([block[...] for block in blocks], axis=0)
        weights = jnp.concatenate(
            [up[e, g] for e in range(up.shape[0]) for g in range(2)], axis=1
        )
        pre[...] += jnp.dot(rows, weights, preferred_element_type=jnp.float32)

    @pl.when(step == STEPS - 1)
    def _():
        gate_rows = jnp.concatenate([ref[...] for ref in gate_refs], axis=0)
        gates = jnp.dot(gate_rows, pick[...], preferred_element_type=jnp.float32)
        for e in range(up.shape[0]):
            gate_pre = pre[:, 2 * e * units : (2 * e + 1) * units]
            up_pre = pre[:, (2 * e + 1) * units : (2 * e + 2) * units]
            value = gate_pre / (1.0 + jnp.exp(-gate_pre)) * up_pre * gates[:, e : e + 1]
            act[:, e * units : (e + 1) * units] = value.astype(jnp.bfloat16)

    @pl.when(step >= STEPS)
    def _():
        result = jnp.dot(act[...], down[...], preferred_element_type=jnp.float32).astype(
            jnp.bfloat16
        )
        at = 0
        for out in outs:
            out[...] = result[at : at + out.shape[0]]
            at += out.shape[0]


def run_experts(groups, up, down, pick):
    sizes = tuple(len(group) for group in groups)
    blocks = [block for group in groups for block in group]
    heights = [sum(block.shape[0] for block in group) for group in groups]
    height = sum(heights)
    experts, _, _, units = up.shape
    tile = D // STEPS
    early = lambda i: jnp.minimum(i, STEPS - 1)
    late = lambda i: jnp.maximum(i - STEPS, 0)
    return pl.pallas_call(
        functools.partial(experts_kernel, sizes),
        grid=(2 * STEPS,),
        in_specs=[pl.BlockSpec((b.shape[0], tile), lambda i: (0, early(i))) for b in blocks]
        + [pl.BlockSpec((b.shape[0], GATE_COLS), lambda i: (0, D // GATE_COLS)) for b in blocks]
        + [
            pl.BlockSpec((experts, 2, tile, units), lambda i: (0, 0, early(i), 0)),
            pl.BlockSpec((experts * units, tile), lambda i: (0, late(i))),
            pl.BlockSpec(pick.shape, lambda i: (0, 0)),
        ],
        out_specs=[pl.BlockSpec((h, tile), lambda i: (0, late(i))) for h in heights],
        out_shape=[jax.ShapeDtypeStruct((h, D), jnp.bfloat16) for h in heights],
        scratch_shapes=[
            pltpu.VMEM((height, experts * 2 * units), jnp.float32),
            pltpu.VMEM((height, experts * units), jnp.bfloat16),
        ],
        compiler_params=pltpu.CompilerParams(vmem_limit_bytes=40 * MIB),
        cost_estimate=pl.CostEstimate(
            flops=0, bytes_accessed=4096, transcendentals=0
        ),
    )(*blocks, *blocks, up, down, pick)


def document(positions, doc_ends):
    return jnp.sum((positions[:, None] >= doc_ends[None, :]).astype(jnp.int32), axis=1)


def attention(latent, query, w_uk, w_uv, doc_lengths):
    tokens = latent.shape[0]
    heads = w_uk.shape[0]
    qk_width = NOPE + ROPE
    score_scale = 1.0 / math.sqrt(qk_width)
    doc_ends = jnp.cumsum(doc_lengths)
    ctx = lax.axis_index("ctx")
    x_hi, y, core = ctx // 8, (ctx // 2) % 4, ctx % 2
    blocks, places = [latent], [ctx]
    for by in (0, 1, -1, 2):
        come = (y - by) % 4
        same = [(a, b) for a, b in table(dy=by) if row(a) < row(b)]
        across = [(a, b) for a, b in table(dx=2, dy=by) if a < 64 and row(a) >= row(b)]
        blocks.append(lax.ppermute(latent, BOTH, same + across))
        place = x_hi * 8 + come * 2 + core
        places.append(
            jnp.where(come < y, place, jnp.where(x_hi > 0, place - 8, NOWHERE))
        )
    last = lax.ppermute(
        latent,
        BOTH,
        [(a, b) for a, b in table(dx=2, dy=1, dc=1) if a < 64 and a // 8 % 2 and row(a) < 3],
    )
    (half,) = stack(blocks)
    (piece,) = stack([half, other_core(half), last])
    starts = [place * tokens for place in places]
    starts += [(place + 1 - 2 * core) * tokens for place in places]
    seen = (x_hi > 0) & (core == 0) & (y > 0)
    starts.append(jnp.where(seen, ctx - 9, NOWHERE) * tokens)
    steps = jnp.arange(tokens, dtype=jnp.int32)
    key_pos = (jnp.stack(starts)[:, None] + steps[None, :]).reshape(-1)
    key_doc = document(key_pos, doc_ends)
    q_pos = ctx * tokens + steps
    q_doc = document(q_pos, doc_ends)
    q_rows = query.reshape(tokens, heads, qk_width)
    q_lat = jnp.einsum(
        "thn,hln->htl", q_rows[:, :, :NOPE], w_uk, preferred_element_type=jnp.float32
    ).astype(jnp.bfloat16)
    q_full = jnp.concatenate(
        [q_lat, jnp.transpose(q_rows[:, :, NOPE:], (1, 0, 2))], axis=2
    ).reshape(heads * tokens, LAT + ROPE)
    row_pos = jnp.tile(q_pos, heads)
    row_doc = jnp.tile(q_doc, heads)
    allowed = (row_doc[:, None] == key_doc[None, :]) & (row_pos[:, None] >= key_pos[None, :])
    scores = jnp.dot(q_full, piece.T, preferred_element_type=jnp.float32) * score_scale
    scores = jnp.where(allowed, scores, -1e30)
    row_max = jnp.max(scores, axis=1)
    weights = jnp.where(allowed, jnp.exp(scores - row_max[:, None]), 0.0)
    row_total = jnp.sum(weights, axis=1)
    accumulated = jnp.dot(
        weights.astype(jnp.bfloat16), piece[:, :LAT], preferred_element_type=jnp.float32
    )
    o_lat = (accumulated / row_total[:, None]).astype(jnp.bfloat16).reshape(heads, tokens, LAT)
    head_out = (
        jnp.einsum("htl,hlv->thv", o_lat, w_uv, preferred_element_type=jnp.float32)
        .astype(jnp.bfloat16)
        .reshape(tokens, heads * VDIM)
    )
    return head_out


def body(
    latent,
    query,
    w_uk,
    w_uv,
    w_o,
    residual,
    norm_gain,
    w_in,
    w_out,
    routes,
    gate_weights,
    doc_lengths,
):
    tokens = latent.shape[0]
    count_exp = lax.axis_size("exp")
    local_width = residual.shape[1]
    own = tokens // count_exp
    ctx, exp = lax.axis_index("ctx"), lax.axis_index("exp")
    local_experts = w_in.shape[0]
    units = w_in.shape[3]

    own_routes = lax.dynamic_slice_in_dim(routes, exp * own, own, axis=0)
    own_gates = lax.dynamic_slice_in_dim(gate_weights, exp * own, own, axis=0)
    named = own_routes[:, :, None] == jnp.arange(EXPERTS, dtype=jnp.int32)[None, None, :]
    dense = jnp.sum(jnp.where(named, own_gates[:, :, None], 0.0), axis=1)
    high = lax.reduce_precision(dense, 8, 7)
    high, low = high.astype(jnp.bfloat16), (dense - high).astype(jnp.bfloat16)
    gate_row = jnp.concatenate(
        [high, low, jnp.zeros((own, GATE_COLS - 2 * EXPERTS), jnp.bfloat16)], axis=1
    )
    column = jnp.arange(GATE_COLS, dtype=jnp.int32)[:, None]
    mine = ctx * local_experts + jnp.arange(local_experts, dtype=jnp.int32)[None, :]
    pick = ((column == mine) | (column == mine + EXPERTS)).astype(jnp.bfloat16)

    up = jnp.transpose(w_in, (0, 2, 1, 3))
    down = w_out.reshape(local_experts * units, D)

    def own_and_theirs(groups):
        theirs = [[other_core(block) for block in group] for group in groups]
        return run_experts(theirs + groups, up, down, pick)

    def both_cores(result):
        half = len(result) // 2
        return [
            add_up(here, other_core(there)).astype(jnp.bfloat16)
            for there, here in zip(result[:half], result[half:])
        ]

    head_out = attention(latent, query, w_uk, w_uv, doc_lengths)
    partial = jnp.dot(head_out, w_o, preferred_element_type=jnp.float32).astype(jnp.bfloat16)
    pieces, rest = [], norm_gain
    for _ in range(3):
        pieces.append(lax.reduce_precision(rest, 8, 7))
        rest = rest - pieces[-1]
    gain_block = jnp.stack(pieces + [jnp.zeros_like(rest)]).astype(jnp.bfloat16)
    gain_cols = 4 * local_width // own
    sent = jnp.concatenate(
        [
            partial.reshape(count_exp, own, D),
            residual.reshape(count_exp, own, local_width),
            jnp.broadcast_to(
                gain_block.reshape(1, own, gain_cols), (count_exp, own, gain_cols)
            ),
        ],
        axis=2,
    )
    parts = lax.all_to_all(sent, "exp", split_axis=0, concat_axis=0)
    parts, up = lax.optimization_barrier((parts, up))
    wide = parts[:, :, D : D + local_width].astype(jnp.float32)
    residual_rows = jnp.transpose(wide, (1, 0, 2)).reshape(own, D)
    pieces = parts[:, :, D + local_width :].astype(jnp.float32)
    gain = jnp.sum(pieces.reshape(count_exp, 4, local_width), axis=1).reshape(D)
    hidden = residual_rows + jnp.sum(parts[:, :, :D].astype(jnp.float32), axis=0)
    squares = jnp.mean(hidden * hidden, axis=1, keepdims=True)
    normed = (hidden * lax.rsqrt(squares + epsilon) * gain[None, :]).astype(jnp.bfloat16)
    rows = jnp.concatenate([normed, gate_row], axis=1)

    x_own, x_before, x_after, x_far = ring(rows, "x")
    first, second = stack([x_own, x_before], [x_after, x_far])
    first, second = stack(ring(first, "z"), ring(second, "y"))
    near = first.shape[0] // 2
    before, after = [], []
    for block, axis in ((first, "y"), (second, "z")):
        before.append([shift(block, axis, 1)])
        after.append([shift(block, axis, -1)])
    at_own = own_and_theirs([[first], [second]])
    before, after, at_own = lax.optimization_barrier((before, after, at_own))
    far = [
        [shift(before[i][0][:near], axis, 1), shift(after[i][0][near:], axis, -1)]
        for i, axis in enumerate("yz")
    ]
    at_before = own_and_theirs(before)
    at_after = own_and_theirs(after)
    far, at_before, at_after = lax.optimization_barrier((far, at_before, at_after))
    sum_own = both_cores(at_own)
    sum_before = both_cores(at_before)
    sum_after = both_cores(at_after)
    near_sums = [
        (shift(sum_before[i], axis, -1), shift(sum_after[i], axis, 1))
        for i, axis in enumerate("yz")
    ]
    near_sums, at_far = lax.optimization_barrier((near_sums, own_and_theirs(far)))
    sum_far = both_cores(at_far)
    first, second = [
        add_up(sum_own[i], *near_sums[i], shift(sum_far[i], axis, 2)).astype(jnp.bfloat16)
        for i, axis in enumerate("yz")
    ]
    pair = 2 * own
    first = ring_sum(*[first[i * pair : (i + 1) * pair] for i in range(4)], "z")
    second = ring_sum(*[second[i * pair : (i + 1) * pair] for i in range(4)], "y")
    first, second = first.astype(jnp.bfloat16), second.astype(jnp.bfloat16)
    moe_out = ring_sum(first[:own], first[own:], second[:own], second[own:], "x")
    mixed = (hidden + moe_out).astype(jnp.bfloat16)
    return lax.all_to_all(mixed, "exp", split_axis=1, concat_axis=0, tiled=True)


def solution(mesh):
    placed = (
        P("ctx", None),
        P("ctx", "exp"),
        P("exp", None, None),
        P("exp", None, None),
        P("exp", None),
        P("ctx", "exp"),
        P("exp"),
        P("ctx", None, None, "exp"),
        P("ctx", "exp", None),
        P("ctx", None),
        P("ctx", None),
        P(),
    )
    return jax.shard_map(
        body, mesh=mesh, in_specs=placed, out_specs=P("ctx", "exp"), check_vma=False
    )
```

```python
import functools
import itertools
import math

import jax
import jax.numpy as jnp
from jax import lax
from jax.experimental import pallas as pl
from jax.experimental.pallas import tpu as pltpu
from jax.sharding import PartitionSpec as P

D = 4096
NOPE = 128
ROPE = 64
LAT = 512
VDIM = 128
TOP = 8
EXPERTS = 32
GATE_COLS = 128
BOTH = ("ctx", "exp")
NOWHERE = 64

epsilon = 1e-06


def table(dx=0, dy=0, dz=0, dc=0):
    def at(x, y, z, c):
        return ((x // 2 * 4 + y) * 2 + c) * 8 + z * 2 + x % 2

    return [
        (at(x, y, z, c), at((x + dx) % 4, (y + dy) % 4, (z + dz) % 4, (c + dc) % 2))
        for x, y, z, c in itertools.product(range(4), range(4), range(4), range(2))
    ]


def row(device):
    return device // 16 % 4


def shift(value, axis, by):
    return lax.ppermute(value, BOTH, table(**{"d" + axis: by}))


def other_core(value):
    return shift(value, "c", 1)


def ring(block, axis):
    return [block, shift(block, axis, 1), shift(block, axis, -1), shift(block, axis, 2)]


def add_up(*blocks):
    total = blocks[0].astype(jnp.float32)
    for block in blocks[1:]:
        total = total + block.astype(jnp.float32)
    return total


def ring_sum(own, before, after, far, axis):
    return add_up(own, shift(before, axis, -1), shift(after, axis, 1), shift(far, axis, 2))


MIB = 1024 * 1024


def grouped(refs, sizes):
    found, at = [], 0
    for size in sizes:
        found.append(refs[at : at + size])
        at += size
    return found


def stack_kernel(sizes, *refs):
    count = sum(sizes)
    for group, out in zip(grouped(refs[:count], sizes), refs[count:]):
        at = 0
        for ref in group:
            out[at : at + ref.shape[0], :] = ref[...]
            at += ref.shape[0]


def stack(*groups):
    sizes = tuple(len(group) for group in groups)
    blocks = [block for group in groups for block in group]
    width = blocks[0].shape[1]
    heights = [sum(block.shape[0] for block in group) for group in groups]
    cuts = 3 if width % 384 == 0 else 1
    tile = width // cuts
    return pl.pallas_call(
        functools.partial(stack_kernel, sizes),
        grid=(cuts,),
        in_specs=[pl.BlockSpec((block.shape[0], tile), lambda i: (0, i)) for block in blocks],
        out_specs=[pl.BlockSpec((height, tile), lambda i: (0, i)) for height in heights],
        out_shape=[jax.ShapeDtypeStruct((height, width), jnp.bfloat16) for height in heights],
        compiler_params=pltpu.CompilerParams(vmem_limit_bytes=16 * MIB),
        cost_estimate=pl.CostEstimate(
            flops=0, bytes_accessed=4 * sum(heights) * width, transcendentals=0
        ),
    )(*blocks)


STEPS = 2


def experts_kernel(sizes, *refs):
    count = sum(sizes)
    blocks, gate_refs = refs[:count], refs[count : 2 * count]
    up, down, pick = refs[2 * count : 2 * count + 3]
    outs = refs[2 * count + 3 : 2 * count + 3 + len(sizes)]
    pre, act = refs[2 * count + 3 + len(sizes) :]
    step = pl.program_id(0)
    units = up.shape[3]

    @pl.when(step == 0)
    def _():
        pre[...] = jnp.zeros_like(pre)

    @pl.when(step < STEPS)
    def _():
        rows = jnp.concatenate([block[...] for block in blocks], axis=0)
        weights = jnp.concatenate(
            [up[e, g] for e in range(up.shape[0]) for g in range(2)], axis=1
        )
        pre[...] += jnp.dot(rows, weights, preferred_element_type=jnp.float32)

    @pl.when(step == STEPS - 1)
    def _():
        gate_rows = jnp.concatenate([ref[...] for ref in gate_refs], axis=0)
        gates = jnp.dot(gate_rows, pick[...], preferred_element_type=jnp.float32)
        for e in range(up.shape[0]):
            gate_pre = pre[:, 2 * e * units : (2 * e + 1) * units]
            up_pre = pre[:, (2 * e + 1) * units : (2 * e + 2) * units]
            value = gate_pre / (1.0 + jnp.exp(-gate_pre)) * up_pre * gates[:, e : e + 1]
            act[:, e * units : (e + 1) * units] = value.astype(jnp.bfloat16)

    @pl.when(step >= STEPS)
    def _():
        result = jnp.dot(act[...], down[...], preferred_element_type=jnp.float32).astype(
            jnp.bfloat16
        )
        at = 0
        for out in outs:
            out[...] = result[at : at + out.shape[0]]
            at += out.shape[0]


def run_experts(groups, up, down, pick):
    sizes = tuple(len(group) for group in groups)
    blocks = [block for group in groups for block in group]
    heights = [sum(block.shape[0] for block in group) for group in groups]
    height = sum(heights)
    experts, _, _, units = up.shape
    tile = D // STEPS
    early = lambda i: jnp.minimum(i, STEPS - 1)
    late = lambda i: jnp.maximum(i - STEPS, 0)
    return pl.pallas_call(
        functools.partial(experts_kernel, sizes),
        grid=(2 * STEPS,),
        in_specs=[pl.BlockSpec((b.shape[0], tile), lambda i: (0, early(i))) for b in blocks]
        + [pl.BlockSpec((b.shape[0], GATE_COLS), lambda i: (0, D // GATE_COLS)) for b in blocks]
        + [
            pl.BlockSpec((experts, 2, tile, units), lambda i: (0, 0, early(i), 0)),
            pl.BlockSpec((experts * units, tile), lambda i: (0, late(i))),
            pl.BlockSpec(pick.shape, lambda i: (0, 0)),
        ],
        out_specs=[pl.BlockSpec((h, tile), lambda i: (0, late(i))) for h in heights],
        out_shape=[jax.ShapeDtypeStruct((h, D), jnp.bfloat16) for h in heights],
        scratch_shapes=[
            pltpu.VMEM((height, experts * 2 * units), jnp.float32),
            pltpu.VMEM((height, experts * units), jnp.bfloat16),
        ],
        compiler_params=pltpu.CompilerParams(vmem_limit_bytes=40 * MIB),
        cost_estimate=pl.CostEstimate(
            flops=0, bytes_accessed=4096, transcendentals=0
        ),
    )(*blocks, *blocks, up, down, pick)


def document(positions, doc_ends):
    return jnp.sum((positions[:, None] >= doc_ends[None, :]).astype(jnp.int32), axis=1)


def attention(latent, query, w_uk, w_uv, doc_lengths):
    tokens = latent.shape[0]
    heads = w_uk.shape[0]
    qk_width = NOPE + ROPE
    score_scale = 1.0 / math.sqrt(qk_width)
    doc_ends = jnp.cumsum(doc_lengths)
    ctx = lax.axis_index("ctx")
    x_hi, y, core = ctx // 8, (ctx // 2) % 4, ctx % 2
    blocks, places = [latent], [ctx]
    for by in (0, 1, -1, 2):
        come = (y - by) % 4
        same = [(a, b) for a, b in table(dy=by) if row(a) < row(b)]
        across = [(a, b) for a, b in table(dx=2, dy=by) if a < 64 and row(a) >= row(b)]
        blocks.append(lax.ppermute(latent, BOTH, same + across))
        place = x_hi * 8 + come * 2 + core
        places.append(
            jnp.where(come < y, place, jnp.where(x_hi > 0, place - 8, NOWHERE))
        )
    last = lax.ppermute(
        latent,
        BOTH,
        [(a, b) for a, b in table(dx=2, dy=1, dc=1) if a < 64 and a // 8 % 2 and row(a) < 3],
    )
    (half,) = stack(blocks)
    (piece,) = stack([half, other_core(half), last])
    starts = [place * tokens for place in places]
    starts += [(place + 1 - 2 * core) * tokens for place in places]
    seen = (x_hi > 0) & (core == 0) & (y > 0)
    starts.append(jnp.where(seen, ctx - 9, NOWHERE) * tokens)
    steps = jnp.arange(tokens, dtype=jnp.int32)
    key_pos = (jnp.stack(starts)[:, None] + steps[None, :]).reshape(-1)
    key_doc = document(key_pos, doc_ends)
    q_pos = ctx * tokens + steps
    q_doc = document(q_pos, doc_ends)
    q_rows = query.reshape(tokens, heads, qk_width)
    q_lat = jnp.einsum(
        "thn,hln->htl", q_rows[:, :, :NOPE], w_uk, preferred_element_type=jnp.float32
    ).astype(jnp.bfloat16)
    q_full = jnp.concatenate(
        [q_lat, jnp.transpose(q_rows[:, :, NOPE:], (1, 0, 2))], axis=2
    ).reshape(heads * tokens, LAT + ROPE)
    row_pos = jnp.tile(q_pos, heads)
    row_doc = jnp.tile(q_doc, heads)
    allowed = (row_doc[:, None] == key_doc[None, :]) & (row_pos[:, None] >= key_pos[None, :])
    scores = jnp.dot(q_full, piece.T, preferred_element_type=jnp.float32) * score_scale
    scores = jnp.where(allowed, scores, -1e30)
    row_max = jnp.max(scores, axis=1)
    weights = jnp.where(allowed, jnp.exp(scores - row_max[:, None]), 0.0)
    row_total = jnp.sum(weights, axis=1)
    accumulated = jnp.dot(
        weights.astype(jnp.bfloat16), piece[:, :LAT], preferred_element_type=jnp.float32
    )
    o_lat = (accumulated / row_total[:, None]).astype(jnp.bfloat16).reshape(heads, tokens, LAT)
    head_out = (
        jnp.einsum("htl,hlv->thv", o_lat, w_uv, preferred_element_type=jnp.float32)
        .astype(jnp.bfloat16)
        .reshape(tokens, heads * VDIM)
    )
    return head_out


def body(
    latent,
    query,
    w_uk,
    w_uv,
    w_o,
    residual,
    norm_gain,
    w_in,
    w_out,
    routes,
    gate_weights,
    doc_lengths,
):
    tokens = latent.shape[0]
    count_exp = lax.axis_size("exp")
    local_width = residual.shape[1]
    own = tokens // count_exp
    ctx, exp = lax.axis_index("ctx"), lax.axis_index("exp")
    local_experts = w_in.shape[0]
    units = w_in.shape[3]

    own_routes = lax.dynamic_slice_in_dim(routes, exp * own, own, axis=0)
    own_gates = lax.dynamic_slice_in_dim(gate_weights, exp * own, own, axis=0)
    named = own_routes[:, :, None] == jnp.arange(EXPERTS, dtype=jnp.int32)[None, None, :]
    dense = jnp.sum(jnp.where(named, own_gates[:, :, None], 0.0), axis=1)
    high = lax.reduce_precision(dense, 8, 7)
    high, low = high.astype(jnp.bfloat16), (dense - high).astype(jnp.bfloat16)
    gate_row = jnp.concatenate(
        [high, low, jnp.zeros((own, GATE_COLS - 2 * EXPERTS), jnp.bfloat16)], axis=1
    )
    column = jnp.arange(GATE_COLS, dtype=jnp.int32)[:, None]
    mine = ctx * local_experts + jnp.arange(local_experts, dtype=jnp.int32)[None, :]
    pick = ((column == mine) | (column == mine + EXPERTS)).astype(jnp.bfloat16)

    up = jnp.transpose(w_in, (0, 2, 1, 3))
    down = w_out.reshape(local_experts * units, D)

    def own_and_theirs(groups):
        theirs = [[other_core(block) for block in group] for group in groups]
        return run_experts(theirs + groups, up, down, pick)

    def both_cores(result):
        half = len(result) // 2
        return [
            add_up(here, other_core(there)).astype(jnp.bfloat16)
            for there, here in zip(result[:half], result[half:])
        ]

    head_out = attention(latent, query, w_uk, w_uv, doc_lengths)
    partial = jnp.dot(head_out, w_o, preferred_element_type=jnp.float32).astype(jnp.bfloat16)
    pieces, rest = [], norm_gain
    for _ in range(3):
        pieces.append(lax.reduce_precision(rest, 8, 7))
        rest = rest - pieces[-1]
    gain_block = jnp.stack(pieces + [jnp.zeros_like(rest)]).astype(jnp.bfloat16)
    gain_cols = 4 * local_width // own
    sent = jnp.concatenate(
        [
            partial.reshape(count_exp, own, D),
            residual.reshape(count_exp, own, local_width),
            jnp.broadcast_to(
                gain_block.reshape(1, own, gain_cols), (count_exp, own, gain_cols)
            ),
        ],
        axis=2,
    )
    parts = lax.all_to_all(sent, "exp", split_axis=0, concat_axis=0)
    parts, up = lax.optimization_barrier((parts, up))
    wide = parts[:, :, D : D + local_width].astype(jnp.float32)
    residual_rows = jnp.transpose(wide, (1, 0, 2)).reshape(own, D)
    pieces = parts[:, :, D + local_width :].astype(jnp.float32)
    gain = jnp.sum(pieces.reshape(count_exp, 4, local_width), axis=1).reshape(D)
    hidden = residual_rows + jnp.sum(parts[:, :, :D].astype(jnp.float32), axis=0)
    squares = jnp.mean(hidden * hidden, axis=1, keepdims=True)
    normed = (hidden * lax.rsqrt(squares + epsilon) * gain[None, :]).astype(jnp.bfloat16)
    rows = jnp.concatenate([normed, gate_row], axis=1)

    x_own, x_before, x_after, x_far = ring(rows, "x")
    first, second = stack([x_own, x_before], [x_after, x_far])
    first, second = stack(ring(first, "z"), ring(second, "y"))
    near = first.shape[0] // 2
    before, after = [], []
    for block, axis in ((first, "y"), (second, "z")):
        before.append([shift(block, axis, 1)])
        after.append([shift(block, axis, -1)])
    at_own = own_and_theirs([[first], [second]])
    before, after, at_own = lax.optimization_barrier((before, after, at_own))
    far_low = [shift(before[i][0][:near], axis, 1) for i, axis in enumerate("yz")]
    far_low, after, at_before = lax.optimization_barrier(
        (far_low, after, own_and_theirs(before))
    )
    far_high = [shift(after[i][0][near:], axis, -1) for i, axis in enumerate("yz")]
    far_high, at_after = lax.optimization_barrier((far_high, own_and_theirs(after)))
    far = [list(halves) for halves in zip(far_low, far_high)]
    sum_own = both_cores(at_own)
    sum_before = both_cores(at_before)
    sum_after = both_cores(at_after)
    near_sums = [
        (shift(sum_before[i], axis, -1), shift(sum_after[i], axis, 1))
        for i, axis in enumerate("yz")
    ]
    near_sums, at_far = lax.optimization_barrier((near_sums, own_and_theirs(far)))
    sum_far = both_cores(at_far)
    first, second = [
        add_up(sum_own[i], *near_sums[i], shift(sum_far[i], axis, 2)).astype(jnp.bfloat16)
        for i, axis in enumerate("yz")
    ]
    pair = 2 * own
    first = ring_sum(*[first[i * pair : (i + 1) * pair] for i in range(4)], "z")
    second = ring_sum(*[second[i * pair : (i + 1) * pair] for i in range(4)], "y")
    first, second = first.astype(jnp.bfloat16), second.astype(jnp.bfloat16)
    moe_out = ring_sum(first[:own], first[own:], second[:own], second[own:], "x")
    mixed = (hidden + moe_out).astype(jnp.bfloat16)
    return lax.all_to_all(mixed, "exp", split_axis=1, concat_axis=0, tiled=True)


def solution(mesh):
    placed = (
        P("ctx", None),
        P("ctx", "exp"),
        P("exp", None, None),
        P("exp", None, None),
        P("exp", None),
        P("ctx", "exp"),
        P("exp"),
        P("ctx", None, None, "exp"),
        P("ctx", "exp", None),
        P("ctx", None),
        P("ctx", None),
        P(),
    )
    return jax.shard_map(
        body, mesh=mesh, in_specs=placed, out_specs=P("ctx", "exp"), check_vma=False
    )
```

```python
import functools
import itertools
import math

import jax
import jax.numpy as jnp
from jax import lax
from jax.experimental import pallas as pl
from jax.experimental.pallas import tpu as pltpu
from jax.sharding import PartitionSpec as P

D = 4096
NOPE = 128
ROPE = 64
LAT = 512
VDIM = 128
TOP = 8
EXPERTS = 32
GATE_COLS = 128
BOTH = ("ctx", "exp")
NOWHERE = 64

epsilon = 1e-06


def table(dx=0, dy=0, dz=0, dc=0):
    def at(x, y, z, c):
        return ((x // 2 * 4 + y) * 2 + c) * 8 + z * 2 + x % 2

    return [
        (at(x, y, z, c), at((x + dx) % 4, (y + dy) % 4, (z + dz) % 4, (c + dc) % 2))
        for x, y, z, c in itertools.product(range(4), range(4), range(4), range(2))
    ]


def row(device):
    return device // 16 % 4


def shift(value, axis, by):
    return lax.ppermute(value, BOTH, table(**{"d" + axis: by}))


def other_core(value):
    return shift(value, "c", 1)


def ring(block, axis):
    return [block, shift(block, axis, 1), shift(block, axis, -1), shift(block, axis, 2)]


def add_up(*blocks):
    total = blocks[0].astype(jnp.float32)
    for block in blocks[1:]:
        total = total + block.astype(jnp.float32)
    return total


def ring_sum(own, before, after, far, axis):
    return add_up(own, shift(before, axis, -1), shift(after, axis, 1), shift(far, axis, 2))


MIB = 1024 * 1024


def grouped(refs, sizes):
    found, at = [], 0
    for size in sizes:
        found.append(refs[at : at + size])
        at += size
    return found


def stack_kernel(sizes, *refs):
    count = sum(sizes)
    for group, out in zip(grouped(refs[:count], sizes), refs[count:]):
        at = 0
        for ref in group:
            out[at : at + ref.shape[0], :] = ref[...]
            at += ref.shape[0]


def stack(*groups):
    sizes = tuple(len(group) for group in groups)
    blocks = [block for group in groups for block in group]
    width = blocks[0].shape[1]
    heights = [sum(block.shape[0] for block in group) for group in groups]
    cuts = 3 if width % 384 == 0 else 1
    tile = width // cuts
    return pl.pallas_call(
        functools.partial(stack_kernel, sizes),
        grid=(cuts,),
        in_specs=[pl.BlockSpec((block.shape[0], tile), lambda i: (0, i)) for block in blocks],
        out_specs=[pl.BlockSpec((height, tile), lambda i: (0, i)) for height in heights],
        out_shape=[jax.ShapeDtypeStruct((height, width), jnp.bfloat16) for height in heights],
        compiler_params=pltpu.CompilerParams(vmem_limit_bytes=16 * MIB),
        cost_estimate=pl.CostEstimate(
            flops=0, bytes_accessed=4 * sum(heights) * width, transcendentals=0
        ),
    )(*blocks)


STEPS = 2


def experts_kernel(sizes, *refs):
    count = sum(sizes)
    blocks, gate_refs = refs[:count], refs[count : 2 * count]
    up, down, pick = refs[2 * count : 2 * count + 3]
    outs = refs[2 * count + 3 : 2 * count + 3 + len(sizes)]
    pre, act = refs[2 * count + 3 + len(sizes) :]
    step = pl.program_id(0)
    units = up.shape[3]

    @pl.when(step == 0)
    def _():
        pre[...] = jnp.zeros_like(pre)

    @pl.when(step < STEPS)
    def _():
        rows = jnp.concatenate([block[...] for block in blocks], axis=0)
        weights = jnp.concatenate(
            [up[e, g] for e in range(up.shape[0]) for g in range(2)], axis=1
        )
        pre[...] += jnp.dot(rows, weights, preferred_element_type=jnp.float32)

    @pl.when(step == STEPS - 1)
    def _():
        gate_rows = jnp.concatenate([ref[...] for ref in gate_refs], axis=0)
        gates = jnp.dot(gate_rows, pick[...], preferred_element_type=jnp.float32)
        for e in range(up.shape[0]):
            gate_pre = pre[:, 2 * e * units : (2 * e + 1) * units]
            up_pre = pre[:, (2 * e + 1) * units : (2 * e + 2) * units]
            value = gate_pre / (1.0 + jnp.exp(-gate_pre)) * up_pre * gates[:, e : e + 1]
            act[:, e * units : (e + 1) * units] = value.astype(jnp.bfloat16)

    @pl.when(step >= STEPS)
    def _():
        result = jnp.dot(act[...], down[...], preferred_element_type=jnp.float32).astype(
            jnp.bfloat16
        )
        at = 0
        for out in outs:
            out[...] = result[at : at + out.shape[0]]
            at += out.shape[0]


def run_experts(groups, up, down, pick):
    sizes = tuple(len(group) for group in groups)
    blocks = [block for group in groups for block in group]
    heights = [sum(block.shape[0] for block in group) for group in groups]
    height = sum(heights)
    experts, _, _, units = up.shape
    tile = D // STEPS
    early = lambda i: jnp.minimum(i, STEPS - 1)
    late = lambda i: jnp.maximum(i - STEPS, 0)
    return pl.pallas_call(
        functools.partial(experts_kernel, sizes),
        grid=(2 * STEPS,),
        in_specs=[pl.BlockSpec((b.shape[0], tile), lambda i: (0, early(i))) for b in blocks]
        + [pl.BlockSpec((b.shape[0], GATE_COLS), lambda i: (0, D // GATE_COLS)) for b in blocks]
        + [
            pl.BlockSpec((experts, 2, tile, units), lambda i: (0, 0, early(i), 0)),
            pl.BlockSpec((experts * units, tile), lambda i: (0, late(i))),
            pl.BlockSpec(pick.shape, lambda i: (0, 0)),
        ],
        out_specs=[pl.BlockSpec((h, tile), lambda i: (0, late(i))) for h in heights],
        out_shape=[jax.ShapeDtypeStruct((h, D), jnp.bfloat16) for h in heights],
        scratch_shapes=[
            pltpu.VMEM((height, experts * 2 * units), jnp.float32),
            pltpu.VMEM((height, experts * units), jnp.bfloat16),
        ],
        compiler_params=pltpu.CompilerParams(vmem_limit_bytes=40 * MIB),
        cost_estimate=pl.CostEstimate(
            flops=0, bytes_accessed=4096, transcendentals=0
        ),
    )(*blocks, *blocks, up, down, pick)


def document(positions, doc_ends):
    return jnp.sum((positions[:, None] >= doc_ends[None, :]).astype(jnp.int32), axis=1)


def attention(latent, query, w_uk, w_uv, doc_lengths):
    tokens = latent.shape[0]
    heads = w_uk.shape[0]
    qk_width = NOPE + ROPE
    score_scale = 1.0 / math.sqrt(qk_width)
    doc_ends = jnp.cumsum(doc_lengths)
    ctx = lax.axis_index("ctx")
    x_hi, y, core = ctx // 8, (ctx // 2) % 4, ctx % 2
    blocks, places = [latent], [ctx]
    for by in (0, 1, -1, 2):
        come = (y - by) % 4
        same = [(a, b) for a, b in table(dy=by) if row(a) < row(b)]
        across = [(a, b) for a, b in table(dx=2, dy=by) if a < 64 and row(a) >= row(b)]
        blocks.append(lax.ppermute(latent, BOTH, same + across))
        place = x_hi * 8 + come * 2 + core
        places.append(
            jnp.where(come < y, place, jnp.where(x_hi > 0, place - 8, NOWHERE))
        )
    last = lax.ppermute(
        latent,
        BOTH,
        [(a, b) for a, b in table(dx=2, dy=1, dc=1) if a < 64 and a // 8 % 2 and row(a) < 3],
    )
    (half,) = stack(blocks)
    (piece,) = stack([half, other_core(half), last])
    starts = [place * tokens for place in places]
    starts += [(place + 1 - 2 * core) * tokens for place in places]
    seen = (x_hi > 0) & (core == 0) & (y > 0)
    starts.append(jnp.where(seen, ctx - 9, NOWHERE) * tokens)
    steps = jnp.arange(tokens, dtype=jnp.int32)
    key_pos = (jnp.stack(starts)[:, None] + steps[None, :]).reshape(-1)
    key_doc = document(key_pos, doc_ends)
    q_pos = ctx * tokens + steps
    q_doc = document(q_pos, doc_ends)
    q_rows = query.reshape(tokens, heads, qk_width)
    q_lat = jnp.einsum(
        "thn,hln->htl", q_rows[:, :, :NOPE], w_uk, preferred_element_type=jnp.float32
    ).astype(jnp.bfloat16)
    q_full = jnp.concatenate(
        [q_lat, jnp.transpose(q_rows[:, :, NOPE:], (1, 0, 2))], axis=2
    ).reshape(heads * tokens, LAT + ROPE)
    row_pos = jnp.tile(q_pos, heads)
    row_doc = jnp.tile(q_doc, heads)
    allowed = (row_doc[:, None] == key_doc[None, :]) & (row_pos[:, None] >= key_pos[None, :])
    scores = jnp.dot(q_full, piece.T, preferred_element_type=jnp.float32) * score_scale
    scores = jnp.where(allowed, scores, -1e30)
    row_max = jnp.max(scores, axis=1)
    weights = jnp.where(allowed, jnp.exp(scores - row_max[:, None]), 0.0)
    row_total = jnp.sum(weights, axis=1)
    accumulated = jnp.dot(
        weights.astype(jnp.bfloat16), piece[:, :LAT], preferred_element_type=jnp.float32
    )
    o_lat = (accumulated / row_total[:, None]).astype(jnp.bfloat16).reshape(heads, tokens, LAT)
    head_out = (
        jnp.einsum("htl,hlv->thv", o_lat, w_uv, preferred_element_type=jnp.float32)
        .astype(jnp.bfloat16)
        .reshape(tokens, heads * VDIM)
    )
    return head_out


def body(
    latent,
    query,
    w_uk,
    w_uv,
    w_o,
    residual,
    norm_gain,
    w_in,
    w_out,
    routes,
    gate_weights,
    doc_lengths,
):
    tokens = latent.shape[0]
    count_exp = lax.axis_size("exp")
    local_width = residual.shape[1]
    own = tokens // count_exp
    ctx, exp = lax.axis_index("ctx"), lax.axis_index("exp")
    local_experts = w_in.shape[0]
    units = w_in.shape[3]

    own_routes = lax.dynamic_slice_in_dim(routes, exp * own, own, axis=0)
    own_gates = lax.dynamic_slice_in_dim(gate_weights, exp * own, own, axis=0)
    named = own_routes[:, :, None] == jnp.arange(EXPERTS, dtype=jnp.int32)[None, None, :]
    dense = jnp.sum(jnp.where(named, own_gates[:, :, None], 0.0), axis=1)
    high = lax.reduce_precision(dense, 8, 7)
    high, low = high.astype(jnp.bfloat16), (dense - high).astype(jnp.bfloat16)
    gate_row = jnp.concatenate(
        [high, low, jnp.zeros((own, GATE_COLS - 2 * EXPERTS), jnp.bfloat16)], axis=1
    )
    column = jnp.arange(GATE_COLS, dtype=jnp.int32)[:, None]
    mine = ctx * local_experts + jnp.arange(local_experts, dtype=jnp.int32)[None, :]
    pick = ((column == mine) | (column == mine + EXPERTS)).astype(jnp.bfloat16)

    up = jnp.transpose(w_in, (0, 2, 1, 3))
    down = w_out.reshape(local_experts * units, D)

    def own_and_theirs(groups):
        theirs = [[other_core(block) for block in group] for group in groups]
        return run_experts(theirs + groups, up, down, pick)

    def both_cores(result):
        half = len(result) // 2
        return [
            add_up(here, other_core(there)).astype(jnp.bfloat16)
            for there, here in zip(result[:half], result[half:])
        ]

    head_out = attention(latent, query, w_uk, w_uv, doc_lengths)
    partial = jnp.dot(head_out, w_o, preferred_element_type=jnp.float32).astype(jnp.bfloat16)
    pieces, rest = [], norm_gain
    for _ in range(3):
        pieces.append(lax.reduce_precision(rest, 8, 7))
        rest = rest - pieces[-1]
    gain_block = jnp.stack(pieces + [jnp.zeros_like(rest)]).astype(jnp.bfloat16)
    gain_cols = 4 * local_width // own
    sent = jnp.concatenate(
        [
            partial.reshape(count_exp, own, D),
            residual.reshape(count_exp, own, local_width),
            jnp.broadcast_to(
                gain_block.reshape(1, own, gain_cols), (count_exp, own, gain_cols)
            ),
        ],
        axis=2,
    )
    parts = lax.all_to_all(sent, "exp", split_axis=0, concat_axis=0)
    parts, up = lax.optimization_barrier((parts, up))
    wide = parts[:, :, D : D + local_width].astype(jnp.float32)
    residual_rows = jnp.transpose(wide, (1, 0, 2)).reshape(own, D)
    pieces = parts[:, :, D + local_width :].astype(jnp.float32)
    gain = jnp.sum(pieces.reshape(count_exp, 4, local_width), axis=1).reshape(D)
    hidden = residual_rows + jnp.sum(parts[:, :, :D].astype(jnp.float32), axis=0)
    squares = jnp.mean(hidden * hidden, axis=1, keepdims=True)
    normed = (hidden * lax.rsqrt(squares + epsilon) * gain[None, :]).astype(jnp.bfloat16)
    rows = jnp.concatenate([normed, gate_row], axis=1)

    x_own, x_before, x_after, x_far = ring(rows, "x")
    first, second = stack([x_own, x_before], [x_after, x_far])
    first, second = stack(ring(first, "z"), ring(second, "y"))
    near = first.shape[0] // 2
    before, after = [], []
    for block, axis in ((first, "y"), (second, "z")):
        before.append([shift(block, axis, 1)])
        after.append([shift(block, axis, -1)])
    at_own = own_and_theirs([[first], [second]])
    before, after, at_own = lax.optimization_barrier((before, after, at_own))
    far_low = [shift(before[i][0][:near], axis, 1) for i, axis in enumerate("yz")]
    far_low, after, at_before = lax.optimization_barrier(
        (far_low, after, own_and_theirs(before))
    )
    far_high = [shift(after[i][0][near:], axis, -1) for i, axis in enumerate("yz")]
    far_high, at_after = lax.optimization_barrier((far_high, own_and_theirs(after)))
    far = [list(halves) for halves in zip(far_low, far_high)]
    sum_own = both_cores(at_own)
    sum_before = both_cores(at_before)
    sum_after = both_cores(at_after)
    back_before = [shift(sum_before[i], axis, -1) for i, axis in enumerate("yz")]
    back_after = [shift(sum_after[i], axis, 1) for i, axis in enumerate("yz")]
    at_far = own_and_theirs(far)
    back_before, at_far = lax.optimization_barrier((back_before, at_far))
    sum_far = both_cores(at_far)
    first, second = [
        add_up(sum_own[i], back_before[i], back_after[i], shift(sum_far[i], axis, 2)).astype(jnp.bfloat16)
        for i, axis in enumerate("yz")
    ]
    pair = 2 * own
    first = ring_sum(*[first[i * pair : (i + 1) * pair] for i in range(4)], "z")
    second = ring_sum(*[second[i * pair : (i + 1) * pair] for i in range(4)], "y")
    first, second = first.astype(jnp.bfloat16), second.astype(jnp.bfloat16)
    moe_out = ring_sum(first[:own], first[own:], second[:own], second[own:], "x")
    mixed = (hidden + moe_out).astype(jnp.bfloat16)
    return lax.all_to_all(mixed, "exp", split_axis=1, concat_axis=0, tiled=True)


def solution(mesh):
    placed = (
        P("ctx", None),
        P("ctx", "exp"),
        P("exp", None, None),
        P("exp", None, None),
        P("exp", None),
        P("ctx", "exp"),
        P("exp"),
        P("ctx", None, None, "exp"),
        P("ctx", "exp", None),
        P("ctx", None),
        P("ctx", None),
        P(),
    )
    return jax.shard_map(
        body, mesh=mesh, in_specs=placed, out_specs=P("ctx", "exp"), check_vma=False
    )
```

```python
import functools
import itertools
import math

import jax
import jax.numpy as jnp
from jax import lax
from jax.experimental import pallas as pl
from jax.experimental.pallas import tpu as pltpu
from jax.sharding import PartitionSpec as P

D = 4096
NOPE = 128
ROPE = 64
LAT = 512
VDIM = 128
TOP = 8
EXPERTS = 32
GATE_COLS = 128
BOTH = ("ctx", "exp")
NOWHERE = 64

epsilon = 1e-06


def table(dx=0, dy=0, dz=0, dc=0):
    def at(x, y, z, c):
        return ((x // 2 * 4 + y) * 2 + c) * 8 + z * 2 + x % 2

    return [
        (at(x, y, z, c), at((x + dx) % 4, (y + dy) % 4, (z + dz) % 4, (c + dc) % 2))
        for x, y, z, c in itertools.product(range(4), range(4), range(4), range(2))
    ]


def row(device):
    return device // 16 % 4


def shift(value, axis, by):
    return lax.ppermute(value, BOTH, table(**{"d" + axis: by}))


def other_core(value):
    return shift(value, "c", 1)


def ring(block, axis):
    return [block, shift(block, axis, 1), shift(block, axis, -1), shift(block, axis, 2)]


def add_up(*blocks):
    total = blocks[0].astype(jnp.float32)
    for block in blocks[1:]:
        total = total + block.astype(jnp.float32)
    return total


def ring_sum(own, before, after, far, axis):
    return add_up(own, shift(before, axis, -1), shift(after, axis, 1), shift(far, axis, 2))


MIB = 1024 * 1024


def grouped(refs, sizes):
    found, at = [], 0
    for size in sizes:
        found.append(refs[at : at + size])
        at += size
    return found


def stack_kernel(sizes, *refs):
    count = sum(sizes)
    for group, out in zip(grouped(refs[:count], sizes), refs[count:]):
        at = 0
        for ref in group:
            out[at : at + ref.shape[0], :] = ref[...]
            at += ref.shape[0]


def stack(*groups):
    sizes = tuple(len(group) for group in groups)
    blocks = [block for group in groups for block in group]
    width = blocks[0].shape[1]
    heights = [sum(block.shape[0] for block in group) for group in groups]
    cuts = 3 if width % 384 == 0 else 1
    tile = width // cuts
    return pl.pallas_call(
        functools.partial(stack_kernel, sizes),
        grid=(cuts,),
        in_specs=[pl.BlockSpec((block.shape[0], tile), lambda i: (0, i)) for block in blocks],
        out_specs=[pl.BlockSpec((height, tile), lambda i: (0, i)) for height in heights],
        out_shape=[jax.ShapeDtypeStruct((height, width), jnp.bfloat16) for height in heights],
        compiler_params=pltpu.CompilerParams(vmem_limit_bytes=16 * MIB),
        cost_estimate=pl.CostEstimate(
            flops=0, bytes_accessed=4 * sum(heights) * width, transcendentals=0
        ),
    )(*blocks)


STEPS = 2


def experts_kernel(sizes, *refs):
    count = sum(sizes)
    blocks, gate_refs = refs[:count], refs[count : 2 * count]
    up, down, pick = refs[2 * count : 2 * count + 3]
    outs = refs[2 * count + 3 : 2 * count + 3 + len(sizes)]
    pre, act = refs[2 * count + 3 + len(sizes) :]
    step = pl.program_id(0)
    units = up.shape[3]

    @pl.when(step == 0)
    def _():
        pre[...] = jnp.zeros_like(pre)

    @pl.when(step < STEPS)
    def _():
        rows = jnp.concatenate([block[...] for block in blocks], axis=0)
        weights = jnp.concatenate(
            [up[e, g] for e in range(up.shape[0]) for g in range(2)], axis=1
        )
        pre[...] += jnp.dot(rows, weights, preferred_element_type=jnp.float32)

    @pl.when(step == STEPS - 1)
    def _():
        gate_rows = jnp.concatenate([ref[...] for ref in gate_refs], axis=0)
        gates = jnp.dot(gate_rows, pick[...], preferred_element_type=jnp.float32)
        for e in range(up.shape[0]):
            gate_pre = pre[:, 2 * e * units : (2 * e + 1) * units]
            up_pre = pre[:, (2 * e + 1) * units : (2 * e + 2) * units]
            value = gate_pre / (1.0 + jnp.exp(-gate_pre)) * up_pre * gates[:, e : e + 1]
            act[:, e * units : (e + 1) * units] = value.astype(jnp.bfloat16)

    @pl.when(step >= STEPS)
    def _():
        result = jnp.dot(act[...], down[...], preferred_element_type=jnp.float32).astype(
            jnp.bfloat16
        )
        at = 0
        for out in outs:
            out[...] = result[at : at + out.shape[0]]
            at += out.shape[0]


def run_experts(groups, up, down, pick):
    sizes = tuple(len(group) for group in groups)
    blocks = [block for group in groups for block in group]
    heights = [sum(block.shape[0] for block in group) for group in groups]
    height = sum(heights)
    experts, _, _, units = up.shape
    tile = D // STEPS
    early = lambda i: jnp.minimum(i, STEPS - 1)
    late = lambda i: jnp.maximum(i - STEPS, 0)
    return pl.pallas_call(
        functools.partial(experts_kernel, sizes),
        grid=(2 * STEPS,),
        in_specs=[pl.BlockSpec((b.shape[0], tile), lambda i: (0, early(i))) for b in blocks]
        + [pl.BlockSpec((b.shape[0], GATE_COLS), lambda i: (0, D // GATE_COLS)) for b in blocks]
        + [
            pl.BlockSpec((experts, 2, tile, units), lambda i: (0, 0, early(i), 0)),
            pl.BlockSpec((experts * units, tile), lambda i: (0, late(i))),
            pl.BlockSpec(pick.shape, lambda i: (0, 0)),
        ],
        out_specs=[pl.BlockSpec((h, tile), lambda i: (0, late(i))) for h in heights],
        out_shape=[jax.ShapeDtypeStruct((h, D), jnp.bfloat16) for h in heights],
        scratch_shapes=[
            pltpu.VMEM((height, experts * 2 * units), jnp.float32),
            pltpu.VMEM((height, experts * units), jnp.bfloat16),
        ],
        compiler_params=pltpu.CompilerParams(vmem_limit_bytes=40 * MIB),
        cost_estimate=pl.CostEstimate(
            flops=0, bytes_accessed=4096, transcendentals=0
        ),
    )(*blocks, *blocks, up, down, pick)


def document(positions, doc_ends):
    return jnp.sum((positions[:, None] >= doc_ends[None, :]).astype(jnp.int32), axis=1)


def attention(latent, query, w_uk, w_uv, doc_lengths):
    tokens = latent.shape[0]
    heads = w_uk.shape[0]
    qk_width = NOPE + ROPE
    score_scale = 1.0 / math.sqrt(qk_width)
    doc_ends = jnp.cumsum(doc_lengths)
    ctx = lax.axis_index("ctx")
    x_hi, y, core = ctx // 8, (ctx // 2) % 4, ctx % 2
    blocks, places = [latent], [ctx]
    for by in (0, 1, -1, 2):
        come = (y - by) % 4
        same = [(a, b) for a, b in table(dy=by) if row(a) < row(b)]
        across = [(a, b) for a, b in table(dx=2, dy=by) if a < 64 and row(a) >= row(b)]
        blocks.append(lax.ppermute(latent, BOTH, same + across))
        place = x_hi * 8 + come * 2 + core
        places.append(
            jnp.where(come < y, place, jnp.where(x_hi > 0, place - 8, NOWHERE))
        )
    last = lax.ppermute(
        latent,
        BOTH,
        [(a, b) for a, b in table(dx=2, dy=1, dc=1) if a < 64 and a // 8 % 2 and row(a) < 3],
    )
    (half,) = stack(blocks)
    (piece,) = stack([half, other_core(half), last])
    starts = [place * tokens for place in places]
    starts += [(place + 1 - 2 * core) * tokens for place in places]
    seen = (x_hi > 0) & (core == 0) & (y > 0)
    starts.append(jnp.where(seen, ctx - 9, NOWHERE) * tokens)
    steps = jnp.arange(tokens, dtype=jnp.int32)
    key_pos = (jnp.stack(starts)[:, None] + steps[None, :]).reshape(-1)
    key_doc = document(key_pos, doc_ends)
    q_pos = ctx * tokens + steps
    q_doc = document(q_pos, doc_ends)
    q_rows = query.reshape(tokens, heads, qk_width)
    q_lat = jnp.einsum(
        "thn,hln->htl", q_rows[:, :, :NOPE], w_uk, preferred_element_type=jnp.float32
    ).astype(jnp.bfloat16)
    q_full = jnp.concatenate(
        [q_lat, jnp.transpose(q_rows[:, :, NOPE:], (1, 0, 2))], axis=2
    ).reshape(heads * tokens, LAT + ROPE)
    row_pos = jnp.tile(q_pos, heads)
    row_doc = jnp.tile(q_doc, heads)
    allowed = (row_doc[:, None] == key_doc[None, :]) & (row_pos[:, None] >= key_pos[None, :])
    scores = jnp.dot(q_full, piece.T, preferred_element_type=jnp.float32) * score_scale
    scores = jnp.where(allowed, scores, -1e30)
    row_max = jnp.max(scores, axis=1)
    weights = jnp.where(allowed, jnp.exp(scores - row_max[:, None]), 0.0)
    row_total = jnp.sum(weights, axis=1)
    accumulated = jnp.dot(
        weights.astype(jnp.bfloat16), piece[:, :LAT], preferred_element_type=jnp.float32
    )
    o_lat = (accumulated / row_total[:, None]).astype(jnp.bfloat16).reshape(heads, tokens, LAT)
    head_out = (
        jnp.einsum("htl,hlv->thv", o_lat, w_uv, preferred_element_type=jnp.float32)
        .astype(jnp.bfloat16)
        .reshape(tokens, heads * VDIM)
    )
    return head_out


def body(
    latent,
    query,
    w_uk,
    w_uv,
    w_o,
    residual,
    norm_gain,
    w_in,
    w_out,
    routes,
    gate_weights,
    doc_lengths,
):
    tokens = latent.shape[0]
    count_exp = lax.axis_size("exp")
    local_width = residual.shape[1]
    own = tokens // count_exp
    ctx, exp = lax.axis_index("ctx"), lax.axis_index("exp")
    local_experts = w_in.shape[0]
    units = w_in.shape[3]

    own_routes = lax.dynamic_slice_in_dim(routes, exp * own, own, axis=0)
    own_gates = lax.dynamic_slice_in_dim(gate_weights, exp * own, own, axis=0)
    named = own_routes[:, :, None] == jnp.arange(EXPERTS, dtype=jnp.int32)[None, None, :]
    dense = jnp.sum(jnp.where(named, own_gates[:, :, None], 0.0), axis=1)
    high = lax.reduce_precision(dense, 8, 7)
    high, low = high.astype(jnp.bfloat16), (dense - high).astype(jnp.bfloat16)
    gate_row = jnp.concatenate(
        [high, low, jnp.zeros((own, GATE_COLS - 2 * EXPERTS), jnp.bfloat16)], axis=1
    )
    column = jnp.arange(GATE_COLS, dtype=jnp.int32)[:, None]
    mine = ctx * local_experts + jnp.arange(local_experts, dtype=jnp.int32)[None, :]
    pick = ((column == mine) | (column == mine + EXPERTS)).astype(jnp.bfloat16)

    up = jnp.transpose(w_in, (0, 2, 1, 3))
    down = w_out.reshape(local_experts * units, D)

    def own_and_theirs(groups):
        theirs = [other_core(block) for group in groups for block in group]
        return run_experts([theirs] + groups, up, down, pick)

    def both_cores(result):
        back = other_core(result[0])
        rows = back.shape[0] // 2
        return [
            add_up(here, back[i * rows : (i + 1) * rows]).astype(jnp.bfloat16)
            for i, here in enumerate(result[1:])
        ]

    head_out = attention(latent, query, w_uk, w_uv, doc_lengths)
    partial = jnp.dot(head_out, w_o, preferred_element_type=jnp.float32).astype(jnp.bfloat16)
    pieces, rest = [], norm_gain
    for _ in range(3):
        pieces.append(lax.reduce_precision(rest, 8, 7))
        rest = rest - pieces[-1]
    gain_block = jnp.stack(pieces + [jnp.zeros_like(rest)]).astype(jnp.bfloat16)
    gain_cols = 4 * local_width // own
    sent = jnp.concatenate(
        [
            partial.reshape(count_exp, own, D),
            residual.reshape(count_exp, own, local_width),
            jnp.broadcast_to(
                gain_block.reshape(1, own, gain_cols), (count_exp, own, gain_cols)
            ),
        ],
        axis=2,
    )
    parts = lax.all_to_all(sent, "exp", split_axis=0, concat_axis=0)
    parts, up = lax.optimization_barrier((parts, up))
    wide = parts[:, :, D : D + local_width].astype(jnp.float32)
    residual_rows = jnp.transpose(wide, (1, 0, 2)).reshape(own, D)
    pieces = parts[:, :, D + local_width :].astype(jnp.float32)
    gain = jnp.sum(pieces.reshape(count_exp, 4, local_width), axis=1).reshape(D)
    hidden = residual_rows + jnp.sum(parts[:, :, :D].astype(jnp.float32), axis=0)
    squares = jnp.mean(hidden * hidden, axis=1, keepdims=True)
    normed = (hidden * lax.rsqrt(squares + epsilon) * gain[None, :]).astype(jnp.bfloat16)
    rows = jnp.concatenate([normed, gate_row], axis=1)

    x_own, x_before, x_after, x_far = ring(rows, "x")
    first, second = stack([x_own, x_before], [x_after, x_far])
    first, second = stack(ring(first, "z"), ring(second, "y"))
    near = first.shape[0] // 2
    before, after = [], []
    for block, axis in ((first, "y"), (second, "z")):
        before.append([shift(block, axis, 1)])
        after.append([shift(block, axis, -1)])
    at_own = own_and_theirs([[first], [second]])
    before, after, at_own = lax.optimization_barrier((before, after, at_own))
    far_low = [shift(before[i][0][:near], axis, 1) for i, axis in enumerate("yz")]
    far_low, after, at_before = lax.optimization_barrier(
        (far_low, after, own_and_theirs(before))
    )
    far_high = [shift(after[i][0][near:], axis, -1) for i, axis in enumerate("yz")]
    far_high, at_after = lax.optimization_barrier((far_high, own_and_theirs(after)))
    far = [list(halves) for halves in zip(far_low, far_high)]
    sum_own = both_cores(at_own)
    sum_before = both_cores(at_before)
    sum_after = both_cores(at_after)
    near_sums = [
        (shift(sum_before[i], axis, -1), shift(sum_after[i], axis, 1))
        for i, axis in enumerate("yz")
    ]
    near_sums, at_far = lax.optimization_barrier((near_sums, own_and_theirs(far)))
    sum_far = both_cores(at_far)
    first, second = [
        add_up(sum_own[i], *near_sums[i], shift(sum_far[i], axis, 2)).astype(jnp.bfloat16)
        for i, axis in enumerate("yz")
    ]
    pair = 2 * own
    first = ring_sum(*[first[i * pair : (i + 1) * pair] for i in range(4)], "z")
    second = ring_sum(*[second[i * pair : (i + 1) * pair] for i in range(4)], "y")
    first, second = first.astype(jnp.bfloat16), second.astype(jnp.bfloat16)
    moe_out = ring_sum(first[:own], first[own:], second[:own], second[own:], "x")
    mixed = (hidden + moe_out).astype(jnp.bfloat16)
    return lax.all_to_all(mixed, "exp", split_axis=1, concat_axis=0, tiled=True)


def solution(mesh):
    placed = (
        P("ctx", None),
        P("ctx", "exp"),
        P("exp", None, None),
        P("exp", None, None),
        P("exp", None),
        P("ctx", "exp"),
        P("exp"),
        P("ctx", None, None, "exp"),
        P("ctx", "exp", None),
        P("ctx", None),
        P("ctx", None),
        P(),
    )
    return jax.shard_map(
        body, mesh=mesh, in_specs=placed, out_specs=P("ctx", "exp"), check_vma=False
    )
```
